256 devices in a mesh: member: 64 (over x, z_hi, y), lon: 4 (over z_lo, core).
Axes of the slice: x: 4, y: 4, z: 8 (z_hi: 4, z_lo: 2; z = z_hi * 2 + z_lo), core: 2. Of those that a mesh axis runs over, the one named last changes fastest.
Arguments:
- air_temp: bfloat16 [64, 4, 64, 2048], P('member', None, None, 'lon'), may hold values from -6 to 6
- air_humid: bfloat16 [64, 4, 64, 2048], P('member', None, None, 'lon'), may hold values from -6 to 6
- wind: bfloat16 [64, 2, 64, 2048], P('member', None, None, 'lon'), may hold values from -6 to 6
- exchange_coef: float32 [64], P('member'), may hold values from 0.5 to 2
- sea_surface_anomaly: float32 [64, 2048], P('member', 'lon'), may hold values from -6 to 6
- sea_ice: float32 [64, 2048], P('member', 'lon'), may hold values from 0 to 1
- current: float32 [2, 64, 2048], P(None, 'member', 'lon'), may hold values from -3 to 3
- surface_mask: int32 [64, 2048], P(None, 'lon'), may hold values from 0 to 2
Outputs:
- deepest_layer_warmth: float32 [64, 64, 2048], P('member', None, 'lon')
- bottom_level_humidity: float32 [64, 64, 2048], P('member', None, 'lon')
- averaged_flux_vector: float32 [4, 64, 2048], P(None, 'member', 'lon')
- sea_surface_temp_updated: float32 [64, 2048], P('member', 'lon')
The draws below stay inside these ranges and needn't reach their ends.
All inputs are finite; a program needn't handle non-finite values.
Results may differ from the reference program's by a relative error of at most 0.0003.
Values sent between devices are 32-bit elements; how exact they have to be, the bound alone decides.
A program may use at most 64 MiB of HBM per device.

```python
import math
import jax
import jax.numpy as jnp
from jax import lax

LAT = 64
LEV = 4
STEPS = 2
MEMBERS = 64
NLON = 2048


def plant(values, stream_key, smallest, largest):
    longest = values.shape.index(max(values.shape))
    spots = []
    for shift in (0, 1):
        where = [jax.random.randint(jax.random.fold_in(stream_key, axis), (), 0, length) for axis, length in enumerate(values.shape)]
        where[longest] = (where[longest] + shift) % values.shape[longest]
        spots.append(tuple(where))
    return values.at[spots[0]].set(smallest).at[spots[1]].set(largest)


def steps_of(stream_key, extent, pieces, low, top_value):
    gain = 1.0
    for dim, blocks in pieces:
        heights = jax.random.uniform(jax.random.fold_in(jax.random.fold_in(stream_key, 6), dim), (blocks,), jnp.float32, low / len(pieces), top_value / len(pieces))
        gain = gain * jnp.repeat(jnp.exp(heights), extent[dim] // blocks).reshape((-1,) + (1,) * (len(extent) - 1 - dim))
    return gain


def normal_values(key, extent, spread, bound, shards=(), dtype=jnp.bfloat16):
    factor_of = steps_of(key, extent, shards, -0.22, 0.18) if shards else 1.0
    drawn = jax.random.normal(key, extent, jnp.float32) * spread * factor_of
    return jnp.minimum(jnp.maximum(drawn, -bound), bound).astype(dtype)


def setup_inputs(seed: int = 0) -> dict:
    keys = jax.random.split(jax.random.key(seed), 9)
    return {
        "air_temp": normal_values(keys[0], (MEMBERS, LEV, LAT, NLON), 1.0, 6.0, ((0, 64), (3, 4))),
        "air_humid": normal_values(keys[1], (MEMBERS, LEV, LAT, NLON), 1.0, 6.0, ((0, 64), (3, 4))),
        "wind": normal_values(keys[2], (MEMBERS, 2, LAT, NLON), 1.0, 6.0, ((0, 64), (3, 4))),
        "exchange_coef": jnp.clip(jnp.exp(math.log(2.0) - 1.3862944 * jax.random.uniform(keys[3], (MEMBERS,), jnp.float32) ** steps_of(keys[3], (MEMBERS,), ((0, 64),), -0.2, 0.2)), 0.5, 2.0),
        "sea_surface_anomaly": normal_values(keys[4], (LAT, NLON), 1.0, 6.0, ((0, 64), (1, 4)), jnp.float32),
        "sea_ice": jnp.clip(1.0 * jax.random.uniform(keys[5], (LAT, NLON), jnp.float32) ** steps_of(keys[5], (LAT, NLON), ((0, 64), (1, 4)), -0.2, 0.2), 0.0, 1.0),
        "current": normal_values(keys[6], (2, LAT, NLON), 0.5, 3.0, ((1, 64), (2, 4)), jnp.float32),
        "surface_mask": plant(jax.random.randint(keys[7], (LAT, NLON), 0, 3), jax.random.fold_in(keys[7], 1), 0, 2).astype(jnp.int32),
    }


diffusion_coef = 0.2
half_courant = 0.1
interval_length = 0.1
vertical_mix = 1.0
advance_ocean_column = 0.5
saturation = 0.5

def vertical(state):
    levels = [state[:, k] for k in range(LEV)]
    diags = [1.0 + 2.0 * vertical_mix for k in range(LEV)]
    diags[0] = 1.0 + vertical_mix
    diags[LEV - 1] = 1.0 + vertical_mix
    cprime = []
    modified_right_hand = []
    for k in range(LEV):
        if k == 0:
            denom = diags[0]
            modified_right_hand.append(levels[0] / denom)
        else:
            denom = diags[k] + vertical_mix * cprime[k - 1]
            modified_right_hand.append((levels[k] + vertical_mix * modified_right_hand[k - 1]) / denom)
        cprime.append(-vertical_mix / denom)
    result = [None] * LEV
    result[LEV - 1] = modified_right_hand[LEV - 1]
    for k in range(LEV - 2, -1, -1):
        result[k] = modified_right_hand[k] - cprime[k] * result[k + 1]
    return jnp.stack(result, axis=1)

def advect(state, east, west, u_wind, v_wind):
    north = jnp.concatenate([state[..., 1:, :], state[..., -1:, :]], axis=-2)
    south = jnp.concatenate([state[..., :1, :], state[..., :-1, :]], axis=-2)
    lapl = east + west + north + south - 4.0 * state
    return state + diffusion_coef * lapl - half_courant * (u_wind * (east - west) + v_wind * (north - south))

def reference(air_temp, air_humid, wind, exchange_coef, sea_surface_anomaly, sea_ice, current, surface_mask):
    seafrac = (surface_mask == 1).astype(jnp.float32) + (surface_mask == 2).astype(jnp.float32) * (1.0 - sea_ice)

    def one(carry, forcing_arguments):
        temp, humid, wnd, coef = forcing_arguments
        state = jnp.stack([temp, humid]).astype(jnp.float32)
        u_wind = wnd[0].astype(jnp.float32)
        v_wind = wnd[1].astype(jnp.float32)
        rel_u = u_wind - current[0]
        rel_v = v_wind - current[1]
        speed = jnp.sqrt(rel_u * rel_u + rel_v * rel_v + 1.0)
        drag = coef * speed * seafrac
        total = jnp.zeros((4, LAT, NLON), jnp.float32)
        for step in range(STEPS):
            east = jnp.roll(state, -1, axis=-1)
            west = jnp.roll(state, 1, axis=-1)
            state = advect(state, east, west, u_wind, v_wind)
            heat = drag * (sea_surface_anomaly - state[0, 0])
            fresh = drag * (saturation * sea_surface_anomaly - state[1, 0])
            state = state.at[0, 0].add(interval_length * heat)
            state = state.at[1, 0].add(interval_length * fresh)
            state = vertical(state)
            total = total + jnp.stack([heat, fresh, drag * rel_u, drag * rel_v])
        return (carry + total, state[:, 0])
    init = jnp.zeros((4, LAT, NLON), jnp.float32)
    summed, surface_fields_list = lax.scan(one, init, (air_temp, air_humid, wind, exchange_coef))
    averaged_flux_vector = summed / jnp.float32(MEMBERS * STEPS)
    sea_surface_temp_updated = sea_surface_anomaly - advance_ocean_column * averaged_flux_vector[0]
    return (surface_fields_list[:, 0], surface_fields_list[:, 1], averaged_flux_vector, sea_surface_temp_updated)
```

```python
import jax
import jax.numpy as jnp
from jax import lax
from jax.experimental import pallas as pl
from jax.experimental.pallas import tpu as pltpu
from jax.sharding import PartitionSpec as P

MESH = pl.DeviceIdType.MESH

LAT = 64
LEV = 4
SLAB = 512
MEMBERS = 64
STEPS = 2

SOLVE = (13.0, 5.0, 2.0, 1.0)
SOLVE_TWICE = (199.0, 125.0, 71.0, 46.0)
C00 = 0.1 * 13.0 / 21.0
D00 = 0.1 * 199.0 / 441.0

ROWS = (LAT + 2) * 8
XY = [(a, b) for a in (2, 1, 3, 0) for b in (2, 1, 3, 0) if a or b]


def kernel(
    temp_hbm, humid_hbm, wind_hbm, coef_ref, sst_hbm, ice_hbm, cur_hbm, mask_hbm,
    out_temp_hbm, out_humid_hbm, flux_ref, sst_new_ref,
    temp, humid, wind, mask, own_cur, own_sst, own_ice,
    x0, xp, xq, bp, bq, a1, a2p, a2q, h1, drag, gap, final, uv, ce, cn, m1, m2,
    gathered, stress, heat, got, part, got_z, edge, edge_in, out_temp, out_humid,
    in_sem, out_sem, z_send, z_recv, xy_send, xy_recv, lon_send, lon_recv, red_send, red_recv, redz_send, redz_recv,
):
    m = lax.axis_index("member")
    lon = lax.axis_index("lon")
    x, z, y = m // 16, (m // 4) % 4, m % 4

    def z_peer(d):
        return (x * 16 + ((z + d) % 4) * 4 + y, lon)

    def xy_peer(a, b):
        return (((x + a) % 4) * 16 + z * 4 + (y + b) % 4, lon)

    def lon_peer(d):
        return (m, (lon + d) % 4)

    loads = [
        pltpu.make_async_copy(src, dst, in_sem.at[i])
        for i, (src, dst) in enumerate(
            [
                (cur_hbm, own_cur),
                (sst_hbm, own_sst),
                (ice_hbm, own_ice),
                (wind_hbm, wind),
                (temp_hbm, temp),
                (humid_hbm, humid),
                (mask_hbm, mask),
            ]
        )
    ]
    for copy in loads:
        copy.start()

    barrier = pltpu.get_barrier_semaphore()
    peers = (
        [z_peer(d) for d in (2, 1, 3)]
        + [xy_peer(a, b) for a, b in XY]
        + [lon_peer(d) for d in (1, 3)]
    )
    for peer in peers:
        pl.semaphore_signal(barrier, inc=1, device_id=peer, device_id_type=MESH)

    def remote(src, dst, send, recv, peer):
        return pltpu.make_async_remote_copy(
            src_ref=src, dst_ref=dst, send_sem=send, recv_sem=recv, device_id=peer, device_id_type=MESH
        )

    sub = lax.broadcasted_iota(jnp.int32, (8, 128), 0)
    lane = lax.broadcasted_iota(jnp.int32, (8, 128), 1)
    first_run = (sub % 4) == 0
    last_run = (sub % 4) == 3
    upper = sub < 4
    lane_first = lane == 0
    lane_last = lane == 127
    slot_of = jnp.where(first_run, lane, jnp.where(last_run, (lane + 1) % 128, -1))

    def spread(ref, start, value):
        for c in range(4):
            ref[pl.ds(start + c, 8, stride=8), :] = value[:, c * 128 : (c + 1) * 128]

    def rows_of(ref, j0, shift=1):
        return ref[pl.ds(pl.multiple_of((j0 + shift) * 8, 8), 64), :].reshape(8, 8, 128)

    def put(ref, j0, value):
        ref[pl.ds(pl.multiple_of((j0 + 1) * 8, 8), 64), :] = value.reshape(64, 128)

    def close(ref):
        ref[0:8, :] = ref[8:16, :]
        ref[ROWS - 8 : ROWS, :] = ref[ROWS - 16 : ROWS - 8, :]

    def pack(packed, j0, tiles):
        for k in range(8):
            packed = jnp.where(slot_of == j0 + k, pltpu.roll(tiles[k], j0 + k, 1), packed)
        return packed

    def merge(i):
        from_west = pltpu.roll(pltpu.roll(edge_in[0, i], 5, 0), 1, 1)
        from_east = pltpu.roll(pltpu.roll(edge_in[1, i], 3, 0), 127, 1)
        return jnp.where(first_run, from_west, from_east)

    def advect(ref, j0, halo):
        centre, north, south = rows_of(ref, j0), rows_of(ref, j0, 2), rows_of(ref, j0, 0)
        eastward, northward = rows_of(ce, j0), rows_of(cn, j0)
        result = []
        for k in range(8):
            c = centre[k]
            own_halo = pltpu.roll(halo, (128 - (j0 + k)) % 128, 1)
            right = pltpu.roll(c, 1, 1)
            left = pltpu.roll(c, 127, 1)
            west = jnp.where(lane_first, jnp.where(first_run, own_halo, pltpu.roll(right, 1, 0)), right)
            east = jnp.where(lane_last, jnp.where(last_run, own_halo, pltpu.roll(left, 7, 0)), left)
            result.append(
                0.2 * c
                + 0.4 * (west + south[k])
                + eastward[k] * (east - west)
                + northward[k] * (north[k] - south[k])
            )
        return jnp.stack(result)

    for copy in loads[3:6]:
        copy.wait()

    def prepare(i, carry):
        r0 = pl.multiple_of(i * 16, 16)
        for f, source in ((0, temp), (1, humid)):
            levels = [source[0, k, pl.ds(r0, 16), :].astype(jnp.float32) for k in range(LEV)]
            once = sum(SOLVE[k] * levels[k] for k in range(LEV)) * (1.0 / 21.0)
            twice = sum(SOLVE_TWICE[k] * levels[k] for k in range(LEV)) * (1.0 / 441.0)
            for h in range(2):
                start = (r0 + 8 * h + 1) * 8 + 4 * f
                for ref, value in ((x0, levels[0]), (xp, once), (xq, twice)):
                    spread(ref, start, value[8 * h : 8 * h + 8])
        u = wind[0, 0, pl.ds(r0, 16), :].astype(jnp.float32)
        v = wind[0, 1, pl.ds(r0, 16), :].astype(jnp.float32)
        for h in range(2):
            start = (r0 + 8 * h + 1) * 8
            own = slice(8 * h, 8 * h + 8)
            spread(uv, start, u[own])
            spread(uv, start + 4, v[own])
            for f in range(2):
                spread(ce, start + 4 * f, 0.2 - 0.1 * u[own])
                spread(cn, start + 4 * f, 0.2 - 0.1 * v[own])
        return carry

    lax.fori_loop(0, LAT // 16, prepare, 0)
    for ref in (x0, xp, xq):
        close(ref)

    def pack_inputs(i, packed):
        j0 = i * 8
        return tuple(pack(t, j0, rows_of(ref, j0)) for t, ref in zip(packed, (x0, xp, xq)))

    zero = jnp.zeros((8, 128), jnp.float32)
    packed = lax.fori_loop(0, LAT // 8, pack_inputs, (zero, zero, zero))
    for i in range(3):
        edge[i] = packed[i]

    for copy in loads[:3]:
        copy.wait()
    gathered[x, z, y, 0:8, :] = own_cur[...]
    gathered[x, z, y, 8:12, :] = own_sst[...]
    gathered[x, z, y, 12:16, :] = own_ice[...]

    pl.semaphore_wait(barrier, len(peers))

    sends = []

    def begin(copy):
        copy.start()
        sends.append(copy)
        return copy

    def forward(i, row_z):
        row = gathered.at[x, row_z, y]
        return [
            begin(remote(row, row, xy_send.at[i, n], xy_recv.at[i, n], xy_peer(a, b)))
            for n, (a, b) in enumerate(XY)
        ]

    def exchange(first, count, turn):
        return [
            begin(
                remote(
                    edge.at[pl.ds(first, count)],
                    edge_in.at[s, pl.ds(first, count)],
                    lon_send.at[turn, s],
                    lon_recv.at[turn, s],
                    lon_peer(d),
                )
            )
            for s, d in ((0, 1), (1, 3))
        ]

    own_row = gathered.at[x, z, y]
    along_z = {
        d: begin(remote(own_row, own_row, z_send.at[d - 1], z_recv.at[d - 1], z_peer(d))) for d in (2, 1, 3)
    }
    halos = exchange(0, 3, 0)
    gathers = forward(0, z)

    loads[6].wait()

    def masks(i, carry):
        r0 = pl.multiple_of(i * 8, 8)
        kind = mask[pl.ds(r0, 8), :]
        start = (r0 + 1) * 8
        sea = jnp.where((kind == 1) | (kind == 2), 1.0, 0.0)
        icy = jnp.where(kind == 2, 1.0, 0.0)
        for f in range(2):
            spread(m1, start + 4 * f, sea)
            spread(m2, start + 4 * f, icy)
        return carry

    lax.fori_loop(0, LAT // 8, masks, 0)

    for copy in halos:
        copy.wait_recv()
    halo = [merge(i) for i in range(3)]

    def first_step(i, packed):
        j0 = i * 8
        put(a1, j0, advect(x0, j0, halo[0]))
        moved_p = advect(xp, j0, halo[1])
        put(bp, j0, moved_p)
        moved_q = advect(xq, j0, halo[2])
        put(bq, j0, moved_q)
        return pack(packed[0], j0, moved_p), pack(packed[1], j0, moved_q)

    packed = lax.fori_loop(0, LAT // 8, first_step, (zero, zero))
    for i in range(2):
        edge[3 + i] = packed[i]
    halos = exchange(3, 2, 1)
    close(bp)
    close(bq)

    for i, d in ((1, 1), (2, 3), (3, 2)):
        along_z[d].wait_recv()
        gathers += forward(i, (z - d + 4) % 4)

    for copy in halos:
        copy.wait_recv()
    halo = [merge(3), merge(4)]

    def second_step(i, carry):
        j0 = i * 8
        put(a2p, j0, advect(bp, j0, halo[0]))
        put(a2q, j0, advect(bq, j0, halo[1]))
        return carry

    lax.fori_loop(0, LAT // 8, second_step, 0)

    for copy in gathers:
        copy.wait_recv()

    coef = coef_ref[0]

    def fluxes(i, packed):
        j0 = i * 8
        ix, iz = i // 2, (i % 2) * 2
        block = gathered[ix, pl.ds(iz, 2)].reshape(8, 16, 128)
        winds, one_step, two_steps = rows_of(uv, j0), rows_of(a1, j0), rows_of(a2p, j0)
        sea, icy = rows_of(m1, j0), rows_of(m2, j0)
        drags, gaps, stresses, heats = [], [], [], []
        for k in range(8):
            rel = winds[k] - block[k, 0:8]
            tile = block[k, 8:16]
            turned = pltpu.roll(tile, 4, 0)
            target = jnp.where(upper, tile, 0.5 * turned)
            ice = jnp.where(upper, turned, tile)
            square = rel * rel
            speed = jnp.sqrt(square + pltpu.roll(square, 4, 0) + 1.0)
            d = coef * speed * (sea[k] - icy[k] * ice)
            drags.append(d)
            stresses.append(2.0 * d * rel)
            gaps.append(target - two_steps[k])
            heats.append(d * (target - one_step[k]))
        put(drag, j0, jnp.stack(drags))
        put(gap, j0, jnp.stack(gaps))
        put(h1, j0, jnp.stack(heats))
        stress[ix, pl.ds(iz, 2)] = jnp.stack(stresses).reshape(2, 4, 8, 128)
        return pack(packed, j0, heats)

    edge[5] = lax.fori_loop(0, LAT // 8, fluxes, zero)
    halos = exchange(5, 1, 2)

    def scatter(k, source):
        return [
            begin(
                remote(
                    source.at[(x + a) % 4, :, (y + b) % 4],
                    got.at[k, n],
                    red_send.at[k, n],
                    red_recv.at[k, n],
                    xy_peer(a, b),
                )
            )
            for n, (a, b) in enumerate(XY)
        ]

    def reduce(k, source, copies):
        total = source[x, :, y]
        for n, copy in enumerate(copies):
            copy.wait_recv()
            total = total + got[k, n]
        part[k] = total
        return [
            begin(
                remote(
                    part.at[k, (z + d) % 4], got_z.at[k, d - 1], redz_send.at[k, d - 1], redz_recv.at[k, d - 1], z_peer(d)
                )
            )
            for d in (2, 1, 3)
        ]

    def owned(k, copies):
        total = part[k, z]
        for copy, d in zip(copies, (2, 1, 3)):
            copy.wait_recv()
            total = total + got_z[k, d - 1]
        return total * (1.0 / (MEMBERS * STEPS))

    stress_copies = scatter(0, stress)
    close(h1)
    for copy in halos:
        copy.wait_recv()
    halo_h = merge(5)

    def last_step(i, carry):
        j0 = i * 8
        ix, iz = i // 2, (i % 2) * 2
        moved = advect(h1, j0, halo_h)
        second = rows_of(drag, j0) * (rows_of(gap, j0) - C00 * moved)
        heat[ix, pl.ds(iz, 2)] = (rows_of(h1, j0) + second).reshape(2, 4, 8, 128)
        put(final, j0, rows_of(a2q, j0) + D00 * moved + C00 * second)
        return carry

    lax.fori_loop(0, LAT // 8, last_step, 0)
    heat_copies = scatter(1, heat)

    def unspread(i, carry):
        r0 = pl.multiple_of(i * 8, 8)
        for f, target in ((0, out_temp), (1, out_humid)):
            for c in range(4):
                target[0, pl.ds(r0, 8), c * 128 : (c + 1) * 128] = final[
                    pl.ds((r0 + 1) * 8 + 4 * f + c, 8, stride=8), :
                ]
        return carry

    lax.fori_loop(0, LAT // 8, unspread, 0)
    stores = [
        pltpu.make_async_copy(out_temp, out_temp_hbm, out_sem.at[0]),
        pltpu.make_async_copy(out_humid, out_humid_hbm, out_sem.at[1]),
    ]
    for copy in stores:
        copy.start()

    stress_z = reduce(0, stress, stress_copies)
    heat_z = reduce(1, heat, heat_copies)
    flux_ref[8:16, :] = owned(0, stress_z)
    warm = owned(1, heat_z)
    flux_ref[0:8, :] = warm
    sst_new_ref[...] = own_sst[...] - 0.5 * warm[0:4, :]
    for copy in stores:
        copy.wait()
    for copy in sends:
        copy.wait_send()


def on_device(
    air_temp, air_humid, wind, exchange_coef, sea_surface_anomaly, sea_ice, current, surface_mask
):
    f32 = jnp.float32
    tall = pltpu.VMEM((ROWS, 128), f32)
    dma = pltpu.SemaphoreType.DMA
    any_space = pl.BlockSpec(memory_space=pl.ANY)
    vmem = pl.BlockSpec(memory_space=pltpu.VMEM)

    out_temp, out_humid, flux, sst_new = pl.pallas_call(
        kernel,
        out_shape=(
            jax.ShapeDtypeStruct((1, LAT, SLAB), f32),
            jax.ShapeDtypeStruct((1, LAT, SLAB), f32),
            jax.ShapeDtypeStruct((16, 128), f32),
            jax.ShapeDtypeStruct((4, 128), f32),
        ),
        in_specs=[any_space] * 3
        + [pl.BlockSpec(memory_space=pltpu.SMEM)]
        + [any_space] * 4,
        out_specs=(any_space, any_space, vmem, vmem),
        scratch_shapes=[
            pltpu.VMEM((1, LEV, LAT, SLAB), jnp.bfloat16),
            pltpu.VMEM((1, LEV, LAT, SLAB), jnp.bfloat16),
            pltpu.VMEM((1, 2, LAT, SLAB), jnp.bfloat16),
            pltpu.VMEM((LAT, SLAB), jnp.int32),
            pltpu.VMEM((8, 128), f32),
            pltpu.VMEM((4, 128), f32),
            pltpu.VMEM((4, 128), f32),
        ]
        + [tall] * 17
        + [
            pltpu.VMEM((4, 4, 4, 16, 128), f32),
            pltpu.VMEM((4, 4, 4, 8, 128), f32),
            pltpu.VMEM((4, 4, 4, 8, 128), f32),
            pltpu.VMEM((2, 15, 4, 8, 128), f32),
            pltpu.VMEM((2, 4, 8, 128), f32),
            pltpu.VMEM((2, 3, 8, 128), f32),
            pltpu.VMEM((6, 8, 128), f32),
            pltpu.VMEM((2, 6, 8, 128), f32),
            pltpu.VMEM((1, LAT, SLAB), f32),
            pltpu.VMEM((1, LAT, SLAB), f32),
            dma((7,)),
            dma((2,)),
            dma((3,)),
            dma((3,)),
            dma((4, 15)),
            dma((4, 15)),
            dma((3, 2)),
            dma((3, 2)),
            dma((2, 15)),
            dma((2, 15)),
            dma((2, 3)),
            dma((2, 3)),
        ],
        compiler_params=pltpu.CompilerParams(
            collective_id=0, has_side_effects=True, vmem_limit_bytes=56 * 2**20
        ),
        cost_estimate=pl.CostEstimate(flops=20_000_000, bytes_accessed=1_200_000, transcendentals=32_768),
    )(
        air_temp,
        air_humid,
        wind,
        exchange_coef,
        sea_surface_anomaly.reshape(4, 128),
        sea_ice.reshape(4, 128),
        current.reshape(8, 128),
        surface_mask,
    )
    return out_temp, out_humid, flux.reshape(4, 1, SLAB), sst_new.reshape(1, SLAB)


def solution(mesh):
    in_specs = (
        P("member", None, None, "lon"),
        P("member", None, None, "lon"),
        P("member", None, None, "lon"),
        P("member"),
        P("member", "lon"),
        P("member", "lon"),
        P(None, "member", "lon"),
        P(None, "lon"),
    )
    out_specs = (
        P("member", None, "lon"),
        P("member", None, "lon"),
        P(None, "member", "lon"),
        P("member", "lon"),
    )
    return jax.shard_map(
        on_device, mesh=mesh, in_specs=in_specs, out_specs=out_specs, check_vma=False
    )
```

```python
import jax
import jax.numpy as jnp
from jax import lax
from jax.experimental import pallas as pl
from jax.experimental.pallas import tpu as pltpu
from jax.sharding import PartitionSpec as P

MESH = pl.DeviceIdType.MESH

LAT = 64
LEV = 4
SLAB = 512
MEMBERS = 64
STEPS = 2

SOLVE = (13.0, 5.0, 2.0, 1.0)
SOLVE_TWICE = (199.0, 125.0, 71.0, 46.0)
C00 = 0.1 * 13.0 / 21.0
D00 = 0.1 * 199.0 / 441.0

ROWS = (LAT + 2) * 8
XY = [(a, b) for a in (2, 1, 3, 0) for b in (2, 1, 3, 0) if a or b]


def kernel(
    temp_hbm, humid_hbm, wind_hbm, coef_hbm, sst_hbm, ice_hbm, cur_hbm, mask_hbm,
    out_temp_hbm, out_humid_hbm, flux_ref, sst_new_ref,
    temp, humid, wind, mask, own_cur, own_sst, own_ice, coef_ref,
    x0, xp, xq, bp, bq, a1, a2p, a2q, h1, drag, gap, final, uv, ce, cn, m1, m2,
    gathered, stress, heat, got, part, got_z, edge, edge_in, out_temp, out_humid,
    in_sem, out_sem, z_send, z_recv, xy_send, xy_recv, lon_send, lon_recv, red_send, red_recv, redz_send, redz_recv,
):
    m = lax.axis_index("member")
    lon = lax.axis_index("lon")
    x, z, y = m // 16, (m // 4) % 4, m % 4

    def z_peer(d):
        return (x * 16 + ((z + d) % 4) * 4 + y, lon)

    def xy_peer(a, b):
        return (((x + a) % 4) * 16 + z * 4 + (y + b) % 4, lon)

    def lon_peer(d):
        return (m, (lon + d) % 4)

    loads = [
        pltpu.make_async_copy(src, dst, in_sem.at[i])
        for i, (src, dst) in enumerate(
            [
                (cur_hbm, own_cur),
                (sst_hbm, own_sst),
                (ice_hbm, own_ice),
                (wind_hbm, wind),
                (temp_hbm, temp),
                (humid_hbm, humid),
                (mask_hbm, mask),
                (coef_hbm, coef_ref),
            ]
        )
    ]
    for copy in loads:
        copy.start()

    barrier = pltpu.get_barrier_semaphore()
    peers = (
        [z_peer(d) for d in (2, 1, 3)]
        + [xy_peer(a, b) for a, b in XY]
        + [lon_peer(d) for d in (1, 3)]
    )
    for peer in peers:
        pl.semaphore_signal(barrier, inc=1, device_id=peer, device_id_type=MESH)

    def remote(src, dst, send, recv, peer):
        return pltpu.make_async_remote_copy(
            src_ref=src, dst_ref=dst, send_sem=send, recv_sem=recv, device_id=peer, device_id_type=MESH
        )

    sub = lax.broadcasted_iota(jnp.int32, (8, 128), 0)
    lane = lax.broadcasted_iota(jnp.int32, (8, 128), 1)
    first_run = (sub % 4) == 0
    last_run = (sub % 4) == 3
    upper = sub < 4
    lane_first = lane == 0
    lane_last = lane == 127
    slot_of = jnp.where(first_run, lane, jnp.where(last_run, (lane + 1) % 128, -1))

    def spread(ref, start, value):
        for c in range(4):
            ref[pl.ds(start + c, 8, stride=8), :] = value[:, c * 128 : (c + 1) * 128]

    def rows_of(ref, j0, shift=1, n=8):
        return ref[pl.ds(pl.multiple_of((j0 + shift) * 8, 8), 8 * n), :].reshape(n, 8, 128)

    def put(ref, j0, value):
        n = value.shape[0]
        ref[pl.ds(pl.multiple_of((j0 + 1) * 8, 8), 8 * n), :] = value.reshape(8 * n, 128)

    def close(ref):
        ref[0:8, :] = ref[8:16, :]
        ref[ROWS - 8 : ROWS, :] = ref[ROWS - 16 : ROWS - 8, :]

    def pack(packed, j0, tiles):
        for k in range(len(tiles)):
            packed = jnp.where(slot_of == j0 + k, pltpu.roll(tiles[k], j0 + k, 1), packed)
        return packed

    def merge(i):
        from_west = pltpu.roll(pltpu.roll(edge_in[0, i], 5, 0), 1, 1)
        from_east = pltpu.roll(pltpu.roll(edge_in[1, i], 3, 0), 127, 1)
        return jnp.where(first_run, from_west, from_east)

    def advect(ref, j0, halo, n=8):
        centre, north, south = (rows_of(ref, j0, shift, n) for shift in (1, 2, 0))
        eastward, northward = rows_of(ce, j0, 1, n), rows_of(cn, j0, 1, n)
        result = []
        for k in range(n):
            c = centre[k]
            own_halo = pltpu.roll(halo, (128 - (j0 + k)) % 128, 1)
            right = pltpu.roll(c, 1, 1)
            left = pltpu.roll(c, 127, 1)
            west = jnp.where(lane_first, jnp.where(first_run, own_halo, pltpu.roll(right, 1, 0)), right)
            east = jnp.where(lane_last, jnp.where(last_run, own_halo, pltpu.roll(left, 7, 0)), left)
            result.append(
                0.2 * c
                + 0.4 * (west + south[k])
                + eastward[k] * (east - west)
                + northward[k] * (north[k] - south[k])
            )
        return jnp.stack(result)

    for copy in loads[:3]:
        copy.wait()
    gathered[x, z, y, 0:8, :] = own_cur[...]
    gathered[x, z, y, 8:12, :] = own_sst[...]
    gathered[x, z, y, 12:16, :] = own_ice[...]

    pl.semaphore_wait(barrier, len(peers))

    sends = []

    def begin(copy):
        copy.start()
        sends.append(copy)
        return copy

    def forward(i, row_z):
        row = gathered.at[x, row_z, y]
        return [
            begin(remote(row, row, xy_send.at[i, n], xy_recv.at[i, n], xy_peer(a, b)))
            for n, (a, b) in enumerate(XY)
        ]

    def exchange(first, count, turn):
        return [
            begin(
                remote(
                    edge.at[pl.ds(first, count)],
                    edge_in.at[s, pl.ds(first, count)],
                    lon_send.at[turn, s],
                    lon_recv.at[turn, s],
                    lon_peer(d),
                )
            )
            for s, d in ((0, 1), (1, 3))
        ]

    own_row = gathered.at[x, z, y]
    along_z = {
        d: begin(remote(own_row, own_row, z_send.at[d - 1], z_recv.at[d - 1], z_peer(d))) for d in (2, 1, 3)
    }
    gathers = [forward(0, z)]

    for copy in loads[3:6]:
        copy.wait()

    def prepare(i, carry):
        r0 = pl.multiple_of(i * 16, 16)
        for f, source in ((0, temp), (1, humid)):
            levels = [source[0, k, pl.ds(r0, 16), :].astype(jnp.float32) for k in range(LEV)]
            once = sum(SOLVE[k] * levels[k] for k in range(LEV)) * (1.0 / 21.0)
            twice = sum(SOLVE_TWICE[k] * levels[k] for k in range(LEV)) * (1.0 / 441.0)
            for h in range(2):
                start = (r0 + 8 * h + 1) * 8 + 4 * f
                for ref, value in ((x0, levels[0]), (xp, once), (xq, twice)):
                    spread(ref, start, value[8 * h : 8 * h + 8])
        u = wind[0, 0, pl.ds(r0, 16), :].astype(jnp.float32)
        v = wind[0, 1, pl.ds(r0, 16), :].astype(jnp.float32)
        for h in range(2):
            start = (r0 + 8 * h + 1) * 8
            own = slice(8 * h, 8 * h + 8)
            spread(uv, start, u[own])
            spread(uv, start + 4, v[own])
            for f in range(2):
                spread(ce, start + 4 * f, 0.2 - 0.1 * u[own])
                spread(cn, start + 4 * f, 0.2 - 0.1 * v[own])
        return carry

    lax.fori_loop(0, LAT // 16, prepare, 0)
    for ref in (x0, xp, xq):
        close(ref)

    def pack_inputs(i, packed):
        j0 = i * 8
        return tuple(pack(t, j0, rows_of(ref, j0)) for t, ref in zip(packed, (x0, xp, xq)))

    zero = jnp.zeros((8, 128), jnp.float32)
    packed = lax.fori_loop(0, LAT // 8, pack_inputs, (zero, zero, zero))
    for i in range(3):
        edge[i] = packed[i]

    halos = exchange(0, 3, 0)
    loads[6].wait()
    loads[7].wait()

    def masks(i, carry):
        r0 = pl.multiple_of(i * 8, 8)
        kind = mask[pl.ds(r0, 8), :]
        start = (r0 + 1) * 8
        sea = jnp.where((kind == 1) | (kind == 2), 1.0, 0.0)
        icy = jnp.where(kind == 2, 1.0, 0.0)
        for f in range(2):
            spread(m1, start + 4 * f, sea)
            spread(m2, start + 4 * f, icy)
        return carry

    lax.fori_loop(0, LAT // 8, masks, 0)

    for i, d in ((1, 1), (2, 3), (3, 2)):
        along_z[d].wait_recv()
        gathers.append(forward(i, (z - d + 4) % 4))

    for copy in halos:
        copy.wait_recv()
    halo = [merge(i) for i in range(3)]

    def first_step(i, packed):
        j0 = i * 8
        put(a1, j0, advect(x0, j0, halo[0]))
        moved_p = advect(xp, j0, halo[1])
        put(bp, j0, moved_p)
        moved_q = advect(xq, j0, halo[2])
        put(bq, j0, moved_q)
        return pack(packed[0], j0, moved_p), pack(packed[1], j0, moved_q)

    packed = lax.fori_loop(0, LAT // 8, first_step, (zero, zero))
    for i in range(2):
        edge[3 + i] = packed[i]
    halos = exchange(3, 2, 1)
    close(bp)
    close(bq)

    for copy in halos:
        copy.wait_recv()
    halo = [merge(3), merge(4)]

    def second_step(i, carry):
        j0 = i * 8
        put(a2p, j0, advect(bp, j0, halo[0]))
        put(a2q, j0, advect(bq, j0, halo[1]))
        return carry

    lax.fori_loop(0, LAT // 8, second_step, 0)

    coef = coef_ref[0]

    def fluxes(row_z):
        def step(ix, packed):
            j0 = ix * 16 + row_z * 4
            block = gathered[ix, row_z]
            winds, one_step, two_steps, sea, icy = (rows_of(ref, j0, 1, 4) for ref in (uv, a1, a2p, m1, m2))
            drags, gaps, stresses, heats = [], [], [], []
            for k in range(4):
                rel = winds[k] - block[k, 0:8]
                tile = block[k, 8:16]
                turned = pltpu.roll(tile, 4, 0)
                target = jnp.where(upper, tile, 0.5 * turned)
                ice = jnp.where(upper, turned, tile)
                square = rel * rel
                speed = jnp.sqrt(square + pltpu.roll(square, 4, 0) + 1.0)
                d = coef * speed * (sea[k] - icy[k] * ice)
                drags.append(d)
                stresses.append(2.0 * d * rel)
                gaps.append(target - two_steps[k])
                heats.append(d * (target - one_step[k]))
            put(drag, j0, jnp.stack(drags))
            put(gap, j0, jnp.stack(gaps))
            put(h1, j0, jnp.stack(heats))
            stress[ix, row_z] = jnp.stack(stresses)
            return pack(packed, j0, heats)

        return step

    packed_h = zero
    for copies, d in zip(gathers, (0, 1, 3, 2)):
        for copy in copies:
            copy.wait_recv()
        packed_h = lax.fori_loop(0, 4, fluxes((z - d + 4) % 4), packed_h)
    edge[5] = packed_h
    halos = exchange(5, 1, 2)

    def scatter(k, source, d):
        return [
            begin(
                remote(
                    source.at[(x + a) % 4, (z + d) % 4, (y + b) % 4],
                    got.at[k, d, n],
                    red_send.at[k, d, n],
                    red_recv.at[k, d, n],
                    xy_peer(a, b),
                )
            )
            for n, (a, b) in enumerate(XY)
        ]

    def reduce(k, source, copies, d):
        total = source[x, (z + d) % 4, y]
        for n, copy in enumerate(copies):
            copy.wait_recv()
            total = total + got[k, d, n]
        part[k, d] = total
        if d:
            return begin(
                remote(part.at[k, d], got_z.at[k, d - 1], redz_send.at[k, d - 1], redz_recv.at[k, d - 1], z_peer(d))
            )

    def owned(k, copies):
        total = part[k, 0]
        for copy, d in zip(copies, (2, 1, 3)):
            copy.wait_recv()
            total = total + got_z[k, d - 1]
        return total * (1.0 / (MEMBERS * STEPS))

    stress_copies = [scatter(0, stress, d) for d in (2, 1, 3, 0)]
    close(h1)
    for copy in halos:
        copy.wait_recv()
    halo_h = merge(5)

    def last_step(row_z):
        def step(ix, carry):
            j0 = ix * 16 + row_z * 4
            moved = advect(h1, j0, halo_h, 4)
            second = rows_of(drag, j0, 1, 4) * (rows_of(gap, j0, 1, 4) - C00 * moved)
            heat[ix, row_z] = rows_of(h1, j0, 1, 4) + second
            put(final, j0, rows_of(a2q, j0, 1, 4) + D00 * moved + C00 * second)
            return carry

        return step

    heat_copies = []
    for d in (2, 1, 3, 0):
        lax.fori_loop(0, 4, last_step((z + d) % 4), 0)
        heat_copies.append(scatter(1, heat, d))

    def unspread(i, carry):
        r0 = pl.multiple_of(i * 8, 8)
        for f, target in ((0, out_temp_hbm), (1, out_humid_hbm)):
            for c in range(4):
                target[0, pl.ds(r0, 8), c * 128 : (c + 1) * 128] = final[
                    pl.ds((r0 + 1) * 8 + 4 * f + c, 8, stride=8), :
                ]
        return carry

    lax.fori_loop(0, LAT // 8, unspread, 0)
    stress_z = [reduce(0, stress, c, d) for c, d in zip(stress_copies, (2, 1, 3, 0))]
    heat_z = [reduce(1, heat, c, d) for c, d in zip(heat_copies, (2, 1, 3, 0))]
    flux_ref[8:16, :] = owned(0, stress_z)
    warm = owned(1, heat_z)
    flux_ref[0:8, :] = warm
    sst_new_ref[...] = own_sst[...] - 0.5 * warm[0:4, :]
    for copy in sends:
        copy.wait_send()


def hand_over(*refs):
    for source, target in zip(refs[:4], refs[4:]):
        target[...] = source[...]


def on_device(
    air_temp, air_humid, wind, exchange_coef, sea_surface_anomaly, sea_ice, current, surface_mask
):
    f32 = jnp.float32
    tall = pltpu.VMEM((ROWS, 128), f32)
    dma = pltpu.SemaphoreType.DMA
    any_space = pl.BlockSpec(memory_space=pl.ANY)
    vmem = pl.BlockSpec(memory_space=pltpu.VMEM)

    out_shape = (
        jax.ShapeDtypeStruct((1, LAT, SLAB), f32),
        jax.ShapeDtypeStruct((1, LAT, SLAB), f32),
        jax.ShapeDtypeStruct((16, 128), f32),
        jax.ShapeDtypeStruct((4, 128), f32),
    )
    results = pl.pallas_call(
        kernel,
        out_shape=tuple(pltpu.VMEM(o.shape, o.dtype) for o in out_shape),
        in_specs=[any_space] * 3 + [pl.BlockSpec(memory_space=pltpu.HBM)] + [any_space] * 4,
        out_specs=(vmem, vmem, vmem, vmem),
        scratch_shapes=[
            pltpu.VMEM((1, LEV, LAT, SLAB), jnp.bfloat16),
            pltpu.VMEM((1, LEV, LAT, SLAB), jnp.bfloat16),
            pltpu.VMEM((1, 2, LAT, SLAB), jnp.bfloat16),
            pltpu.VMEM((LAT, SLAB), jnp.int32),
            pltpu.VMEM((8, 128), f32),
            pltpu.VMEM((4, 128), f32),
            pltpu.VMEM((4, 128), f32),
            pltpu.SMEM((1,), f32),
        ]
        + [tall] * 17
        + [
            pltpu.VMEM((4, 4, 4, 16, 128), f32),
            pltpu.VMEM((4, 4, 4, 8, 128), f32),
            pltpu.VMEM((4, 4, 4, 8, 128), f32),
            pltpu.VMEM((2, 4, 15, 8, 128), f32),
            pltpu.VMEM((2, 4, 8, 128), f32),
            pltpu.VMEM((2, 3, 8, 128), f32),
            pltpu.VMEM((6, 8, 128), f32),
            pltpu.VMEM((2, 6, 8, 128), f32),
            pltpu.VMEM((1, LAT, SLAB), f32),
            pltpu.VMEM((1, LAT, SLAB), f32),
            dma((8,)),
            dma((2,)),
            dma((3,)),
            dma((3,)),
            dma((4, 15)),
            dma((4, 15)),
            dma((3, 2)),
            dma((3, 2)),
            dma((2, 4, 15)),
            dma((2, 4, 15)),
            dma((2, 3)),
            dma((2, 3)),
        ],
        compiler_params=pltpu.CompilerParams(
            collective_id=0, has_side_effects=True, vmem_limit_bytes=56 * 2**20
        ),
        cost_estimate=pl.CostEstimate(flops=20_000_000, bytes_accessed=1_200_000, transcendentals=32_768),
    )(
        air_temp,
        air_humid,
        wind,
        exchange_coef,
        sea_surface_anomaly.reshape(4, 128),
        sea_ice.reshape(4, 128),
        current.reshape(8, 128),
        surface_mask,
    )
    out_temp, out_humid, flux, sst_new = pl.pallas_call(
        hand_over,
        out_shape=out_shape,
        in_specs=[vmem] * 4,
        out_specs=[vmem] * 4,
    )(*[pltpu.with_memory_space_constraint(r, pltpu.VMEM) for r in results])
    return out_temp, out_humid, flux.reshape(4, 1, SLAB), sst_new.reshape(1, SLAB)


def solution(mesh):
    in_specs = (
        P("member", None, None, "lon"),
        P("member", None, None, "lon"),
        P("member", None, None, "lon"),
        P("member"),
        P("member", "lon"),
        P("member", "lon"),
        P(None, "member", "lon"),
        P(None, "lon"),
    )
    out_specs = (
        P("member", None, "lon"),
        P("member", None, "lon"),
        P(None, "member", "lon"),
        P("member", "lon"),
    )
    return jax.shard_map(
        on_device, mesh=mesh, in_specs=in_specs, out_specs=out_specs, check_vma=False
    )
```

```python
import jax
import jax.numpy as jnp
from jax import lax
from jax.experimental import pallas as pl
from jax.experimental.pallas import tpu as pltpu
from jax.sharding import PartitionSpec as P

MESH = pl.DeviceIdType.MESH

LAT = 64
LEV = 4
SLAB = 512
MEMBERS = 64
STEPS = 2

SOLVE = (13.0, 5.0, 2.0, 1.0)
SOLVE_TWICE = (199.0, 125.0, 71.0, 46.0)
C00 = 0.1 * 13.0 / 21.0
D00 = 0.1 * 199.0 / 441.0

ROWS = (LAT + 2) * 8
XY = [(a, b) for a in (2, 1, 3, 0) for b in (2, 1, 3, 0) if a or b]


def kernel(
    temp_hbm, humid_hbm, wind_hbm, coef_hbm, sst_hbm, ice_hbm, cur_hbm, mask_hbm,
    out_temp_hbm, out_humid_hbm, flux_ref, sst_new_ref,
    temp, humid, wind, mask, own_cur, own_sst, own_ice, coef_ref,
    x0, xp, xq, bp, bq, a1, a2p, a2q, h1, drag, gap, final, uv, ce, cn, m1, m2,
    gathered, stress, heat, got, part, got_z, edge, edge_in, out_temp, out_humid,
    in_sem, out_sem, z_send, z_recv, xy_send, xy_recv, lon_send, lon_recv, red_send, red_recv, redz_send, redz_recv,
):
    m = lax.axis_index("member")
    lon = lax.axis_index("lon")
    x, z, y = m // 16, (m // 4) % 4, m % 4

    def z_peer(d):
        return (x * 16 + ((z + d) % 4) * 4 + y, lon)

    def xy_peer(a, b):
        return (((x + a) % 4) * 16 + z * 4 + (y + b) % 4, lon)

    def lon_peer(d):
        return (m, (lon + d) % 4)

    barrier = pltpu.get_barrier_semaphore()
    peers = (
        [z_peer(d) for d in (2, 1, 3)]
        + [xy_peer(a, b) for a, b in XY]
        + [lon_peer(d) for d in (1, 3)]
    )
    for peer in peers:
        pl.semaphore_signal(barrier, inc=1, device_id=peer, device_id_type=MESH)

    loads = [
        pltpu.make_async_copy(src, dst, in_sem.at[i])
        for i, (src, dst) in enumerate(
            [
                (cur_hbm, own_cur),
                (sst_hbm, own_sst),
                (ice_hbm, own_ice),
                (wind_hbm, wind),
                (temp_hbm, temp),
                (humid_hbm, humid),
                (mask_hbm, mask),
                (coef_hbm, coef_ref),
            ]
        )
    ]
    for copy in loads:
        copy.start()

    def remote(src, dst, send, recv, peer):
        return pltpu.make_async_remote_copy(
            src_ref=src, dst_ref=dst, send_sem=send, recv_sem=recv, device_id=peer, device_id_type=MESH
        )

    sub = lax.broadcasted_iota(jnp.int32, (8, 128), 0)
    lane = lax.broadcasted_iota(jnp.int32, (8, 128), 1)
    first_run = (sub % 4) == 0
    last_run = (sub % 4) == 3
    upper = sub < 4
    lane_first = lane == 0
    lane_last = lane == 127
    second_slot_of = jnp.where(first_run, (lane + 127) % 128, jnp.where(last_run, (lane + 2) % 128, -1))
    slot_of = jnp.where(first_run, lane, jnp.where(last_run, (lane + 1) % 128, -1))

    def spread(ref, start, value):
        for c in range(4):
            ref[pl.ds(start + c, 8, stride=8), :] = value[:, c * 128 : (c + 1) * 128]

    def rows_of(ref, j0, shift=1, n=8):
        return ref[pl.ds(pl.multiple_of((j0 + shift) * 8, 8), 8 * n), :].reshape(n, 8, 128)

    def put(ref, j0, value):
        n = value.shape[0]
        ref[pl.ds(pl.multiple_of((j0 + 1) * 8, 8), 8 * n), :] = value.reshape(8 * n, 128)

    def close(ref):
        ref[0:8, :] = ref[8:16, :]
        ref[ROWS - 8 : ROWS, :] = ref[ROWS - 16 : ROWS - 8, :]

    def pack(packed, j0, tiles):
        for k in range(len(tiles)):
            packed = jnp.where(slot_of == j0 + k, pltpu.roll(tiles[k], j0 + k, 1), packed)
        return packed

    def pack_two(packed, second, j0, tiles):
        for k in range(len(tiles)):
            turned = pltpu.roll(tiles[k], j0 + k, 1)
            packed = jnp.where(slot_of == j0 + k, turned, packed)
            second = jnp.where(second_slot_of == j0 + k, turned, second)
        return packed, second

    def align(second):
        return jnp.where(first_run, pltpu.roll(second, 127, 1), pltpu.roll(second, 1, 1))

    def advect_halo(centre, inner, outer, eastward, northward):
        west = jnp.where(first_run, outer, inner)
        east = jnp.where(first_run, inner, outer)
        north = jnp.where(slot_of == LAT - 1, centre, pltpu.roll(centre, 127, 1))
        south = jnp.where(slot_of == 0, centre, pltpu.roll(centre, 1, 1))
        return 0.2 * centre + 0.4 * (west + south) + eastward * (east - west) + northward * (north - south)

    def merge(i):
        from_west = pltpu.roll(pltpu.roll(edge_in[0, i], 5, 0), 1, 1)
        from_east = pltpu.roll(pltpu.roll(edge_in[1, i], 3, 0), 127, 1)
        return jnp.where(first_run, from_west, from_east)

    def advect(ref, j0, halo, n=8):
        centre, north, south = (rows_of(ref, j0, shift, n) for shift in (1, 2, 0))
        eastward, northward = rows_of(ce, j0, 1, n), rows_of(cn, j0, 1, n)
        result = []
        for k in range(n):
            c = centre[k]
            own_halo = pltpu.roll(halo, (128 - (j0 + k)) % 128, 1)
            right = pltpu.roll(c, 1, 1)
            left = pltpu.roll(c, 127, 1)
            west = jnp.where(lane_first, jnp.where(first_run, own_halo, pltpu.roll(right, 1, 0)), right)
            east = jnp.where(lane_last, jnp.where(last_run, own_halo, pltpu.roll(left, 7, 0)), left)
            result.append(
                0.2 * c
                + 0.4 * (west + south[k])
                + eastward[k] * (east - west)
                + northward[k] * (north[k] - south[k])
            )
        return jnp.stack(result)

    for copy in loads[:3]:
        copy.wait()
    gathered[x, z, y, 0:8, :] = own_cur[...]
    gathered[x, z, y, 8:12, :] = own_sst[...]
    gathered[x, z, y, 12:16, :] = own_ice[...]

    pl.semaphore_wait(barrier, len(peers))

    sends = []

    def begin(copy):
        copy.start()
        sends.append(copy)
        return copy

    def forward(i, row_z):
        row = gathered.at[x, row_z, y]
        return [
            begin(remote(row, row, xy_send.at[i, n], xy_recv.at[i, n], xy_peer(a, b)))
            for n, (a, b) in enumerate(XY)
        ]

    def exchange(first, count, turn):
        return [
            begin(
                remote(
                    edge.at[pl.ds(first, count)],
                    edge_in.at[s, pl.ds(first, count)],
                    lon_send.at[turn, s],
                    lon_recv.at[turn, s],
                    lon_peer(d),
                )
            )
            for s, d in ((0, 1), (1, 3))
        ]

    own_row = gathered.at[x, z, y]
    along_z = {
        d: begin(remote(own_row, own_row, z_send.at[d - 1], z_recv.at[d - 1], z_peer(d))) for d in (2, 1, 3)
    }
    gathers = [forward(0, z)]

    for copy in loads[3:6]:
        copy.wait()

    def prepare(i, carry):
        r0 = pl.multiple_of(i * 16, 16)
        for f, source in ((0, temp), (1, humid)):
            levels = [source[0, k, pl.ds(r0, 16), :].astype(jnp.float32) for k in range(LEV)]
            once = sum(SOLVE[k] * levels[k] for k in range(LEV)) * (1.0 / 21.0)
            twice = sum(SOLVE_TWICE[k] * levels[k] for k in range(LEV)) * (1.0 / 441.0)
            for h in range(2):
                start = (r0 + 8 * h + 1) * 8 + 4 * f
                for ref, value in ((x0, levels[0]), (xp, once), (xq, twice)):
                    spread(ref, start, value[8 * h : 8 * h + 8])
        u = wind[0, 0, pl.ds(r0, 16), :].astype(jnp.float32)
        v = wind[0, 1, pl.ds(r0, 16), :].astype(jnp.float32)
        for h in range(2):
            start = (r0 + 8 * h + 1) * 8
            own = slice(8 * h, 8 * h + 8)
            spread(uv, start, u[own])
            spread(uv, start + 4, v[own])
            for f in range(2):
                spread(ce, start + 4 * f, 0.2 - 0.1 * u[own])
                spread(cn, start + 4 * f, 0.2 - 0.1 * v[own])
        return carry

    lax.fori_loop(0, LAT // 16, prepare, 0)
    for ref in (x0, xp, xq):
        close(ref)

    def pack_inputs(i, packed):
        j0 = i * 8
        first, p, p2, q, q2, east, north = packed
        p, p2 = pack_two(p, p2, j0, rows_of(xp, j0))
        q, q2 = pack_two(q, q2, j0, rows_of(xq, j0))
        first, east, north = (
            pack(t, j0, rows_of(ref, j0)) for t, ref in ((first, x0), (east, ce), (north, cn))
        )
        return first, p, p2, q, q2, east, north

    zero = jnp.zeros((8, 128), jnp.float32)
    packed = lax.fori_loop(0, LAT // 8, pack_inputs, (zero,) * 7)
    for i in range(7):
        edge[i] = align(packed[i]) if i in (2, 4) else packed[i]

    halos = exchange(0, 7, 0)
    loads[6].wait()
    loads[7].wait()

    def masks(i, carry):
        r0 = pl.multiple_of(i * 8, 8)
        kind = mask[pl.ds(r0, 8), :]
        start = (r0 + 1) * 8
        sea = jnp.where((kind == 1) | (kind == 2), 1.0, 0.0)
        icy = jnp.where(kind == 2, 1.0, 0.0)
        for f in range(2):
            spread(m1, start + 4 * f, sea)
            spread(m2, start + 4 * f, icy)
        return carry

    lax.fori_loop(0, LAT // 8, masks, 0)

    for i, d in ((1, 1), (2, 3), (3, 2)):
        along_z[d].wait_recv()
        gathers.append(forward(i, (z - d + 4) % 4))

    for copy in halos:
        copy.wait_recv()
    halo = [merge(i) for i in range(7)]
    halo_bp = advect_halo(halo[1], edge[1], halo[2], halo[5], halo[6])
    halo_bq = advect_halo(halo[3], edge[3], halo[4], halo[5], halo[6])

    def first_step(i, carry):
        j0 = i * 8
        put(a1, j0, advect(x0, j0, halo[0]))
        put(bp, j0, advect(xp, j0, halo[1]))
        put(bq, j0, advect(xq, j0, halo[3]))
        return carry

    lax.fori_loop(0, LAT // 8, first_step, 0)
    close(bp)
    close(bq)

    def second_step(i, carry):
        j0 = i * 8
        put(a2p, j0, advect(bp, j0, halo_bp))
        put(a2q, j0, advect(bq, j0, halo_bq))
        return carry

    lax.fori_loop(0, LAT // 8, second_step, 0)

    coef = coef_ref[0]

    def fluxes(row_z):
        def step(ix, packed):
            j0 = ix * 16 + row_z * 4
            block = gathered[ix, row_z]
            winds, one_step, two_steps, sea, icy = (rows_of(ref, j0, 1, 4) for ref in (uv, a1, a2p, m1, m2))
            drags, gaps, stresses, heats = [], [], [], []
            for k in range(4):
                rel = winds[k] - block[k, 0:8]
                tile = block[k, 8:16]
                turned = pltpu.roll(tile, 4, 0)
                target = jnp.where(upper, tile, 0.5 * turned)
                ice = jnp.where(upper, turned, tile)
                square = rel * rel
                speed = jnp.sqrt(square + pltpu.roll(square, 4, 0) + 1.0)
                d = coef * speed * (sea[k] - icy[k] * ice)
                drags.append(d)
                stresses.append(2.0 * d * rel)
                gaps.append(target - two_steps[k])
                heats.append(d * (target - one_step[k]))
            put(drag, j0, jnp.stack(drags))
            put(gap, j0, jnp.stack(gaps))
            put(h1, j0, jnp.stack(heats))
            stress[ix, row_z] = jnp.stack(stresses)
            return pack(packed, j0, heats)

        return step

    packed_h = zero
    for copies, d in zip(gathers, (0, 1, 3, 2)):
        for copy in copies:
            copy.wait_recv()
        packed_h = lax.fori_loop(0, 4, fluxes((z - d + 4) % 4), packed_h, unroll=True)
    edge[7] = packed_h
    halos = exchange(7, 1, 1)

    def scatter(k, source, d):
        return [
            begin(
                remote(
                    source.at[(x + a) % 4, (z + d) % 4, (y + b) % 4],
                    got.at[k, d, n],
                    red_send.at[k, d, n],
                    red_recv.at[k, d, n],
                    xy_peer(a, b),
                )
            )
            for n, (a, b) in enumerate(XY)
        ]

    def reduce(k, source, copies, d):
        total = source[x, (z + d) % 4, y]
        for n, copy in enumerate(copies):
            copy.wait_recv()
            total = total + got[k, d, n]
        part[k, d] = total
        if d:
            return begin(
                remote(part.at[k, d], got_z.at[k, d - 1], redz_send.at[k, d - 1], redz_recv.at[k, d - 1], z_peer(d))
            )

    def owned(k, copies):
        total = part[k, 0]
        for copy, d in zip(copies, (2, 1, 3)):
            copy.wait_recv()
            total = total + got_z[k, d - 1]
        return total * (1.0 / (MEMBERS * STEPS))

    stress_copies = [scatter(0, stress, d) for d in (2, 1, 3, 0)]
    close(h1)
    for copy in halos:
        copy.wait_recv()
    halo_h = merge(7)

    def last_step(row_z):
        def step(ix, carry):
            j0 = ix * 16 + row_z * 4
            moved = advect(h1, j0, halo_h, 4)
            second = rows_of(drag, j0, 1, 4) * (rows_of(gap, j0, 1, 4) - C00 * moved)
            heat[ix, row_z] = rows_of(h1, j0, 1, 4) + second
            put(final, j0, rows_of(a2q, j0, 1, 4) + D00 * moved + C00 * second)
            return carry

        return step

    heat_copies = []
    for d in (2, 1, 3, 0):
        lax.fori_loop(0, 4, last_step((z + d) % 4), 0, unroll=True)
        heat_copies.append(scatter(1, heat, d))

    def unspread(i, carry):
        r0 = pl.multiple_of(i * 8, 8)
        for f, target in ((0, out_temp_hbm), (1, out_humid_hbm)):
            for c in range(4):
                target[0, pl.ds(r0, 8), c * 128 : (c + 1) * 128] = final[
                    pl.ds((r0 + 1) * 8 + 4 * f + c, 8, stride=8), :
                ]
        return carry

    lax.fori_loop(0, LAT // 8, unspread, 0)
    stress_z = [reduce(0, stress, c, d) for c, d in zip(stress_copies, (2, 1, 3, 0))]
    early, sends[:] = sends[:], []
    for copy in early:
        copy.wait_send()
    heat_z = [reduce(1, heat, c, d) for c, d in zip(heat_copies, (2, 1, 3, 0))]
    flux_ref[8:16, :] = owned(0, stress_z)
    warm = owned(1, heat_z)
    flux_ref[0:8, :] = warm
    sst_new_ref[...] = own_sst[...] - 0.5 * warm[0:4, :]
    for copy in sends:
        copy.wait_send()


def hand_over(*refs):
    for source, target in zip(refs[:4], refs[4:]):
        target[...] = source[...]


def on_device(
    air_temp, air_humid, wind, exchange_coef, sea_surface_anomaly, sea_ice, current, surface_mask
):
    f32 = jnp.float32
    tall = pltpu.VMEM((ROWS, 128), f32)
    dma = pltpu.SemaphoreType.DMA
    any_space = pl.BlockSpec(memory_space=pl.ANY)
    vmem = pl.BlockSpec(memory_space=pltpu.VMEM)

    out_shape = (
        jax.ShapeDtypeStruct((1, LAT, SLAB), f32),
        jax.ShapeDtypeStruct((1, LAT, SLAB), f32),
        jax.ShapeDtypeStruct((16, 128), f32),
        jax.ShapeDtypeStruct((4, 128), f32),
    )
    results = pl.pallas_call(
        kernel,
        out_shape=tuple(pltpu.VMEM(o.shape, o.dtype) for o in out_shape),
        in_specs=[any_space] * 3 + [pl.BlockSpec(memory_space=pltpu.HBM)] + [any_space] * 4,
        out_specs=(vmem, vmem, vmem, vmem),
        scratch_shapes=[
            pltpu.VMEM((1, LEV, LAT, SLAB), jnp.bfloat16),
            pltpu.VMEM((1, LEV, LAT, SLAB), jnp.bfloat16),
            pltpu.VMEM((1, 2, LAT, SLAB), jnp.bfloat16),
            pltpu.VMEM((LAT, SLAB), jnp.int32),
            pltpu.VMEM((8, 128), f32),
            pltpu.VMEM((4, 128), f32),
            pltpu.VMEM((4, 128), f32),
            pltpu.SMEM((1,), f32),
        ]
        + [tall] * 17
        + [
            pltpu.VMEM((4, 4, 4, 16, 128), f32),
            pltpu.VMEM((4, 4, 4, 8, 128), f32),
            pltpu.VMEM((4, 4, 4, 8, 128), f32),
            pltpu.VMEM((2, 4, 15, 8, 128), f32),
            pltpu.VMEM((2, 4, 8, 128), f32),
            pltpu.VMEM((2, 3, 8, 128), f32),
            pltpu.VMEM((8, 8, 128), f32),
            pltpu.VMEM((2, 8, 8, 128), f32),
            pltpu.VMEM((1, LAT, SLAB), f32),
            pltpu.VMEM((1, LAT, SLAB), f32),
            dma((8,)),
            dma((2,)),
            dma((3,)),
            dma((3,)),
            dma((4, 15)),
            dma((4, 15)),
            dma((2, 2)),
            dma((2, 2)),
            dma((2, 4, 15)),
            dma((2, 4, 15)),
            dma((2, 3)),
            dma((2, 3)),
        ],
        compiler_params=pltpu.CompilerParams(
            collective_id=0, has_side_effects=True, vmem_limit_bytes=56 * 2**20
        ),
        cost_estimate=pl.CostEstimate(flops=20_000_000, bytes_accessed=1_200_000, transcendentals=32_768),
    )(
        air_temp,
        air_humid,
        wind,
        exchange_coef,
        sea_surface_anomaly.reshape(4, 128),
        sea_ice.reshape(4, 128),
        current.reshape(8, 128),
        surface_mask,
    )
    out_temp, out_humid, flux, sst_new = pl.pallas_call(
        hand_over,
        out_shape=out_shape,
        in_specs=[vmem] * 4,
        out_specs=[vmem] * 4,
    )(*[pltpu.with_memory_space_constraint(r, pltpu.VMEM) for r in results])
    return out_temp, out_humid, flux.reshape(4, 1, SLAB), sst_new.reshape(1, SLAB)


def solution(mesh):
    in_specs = (
        P("member", None, None, "lon"),
        P("member", None, None, "lon"),
        P("member", None, None, "lon"),
        P("member"),
        P("member", "lon"),
        P("member", "lon"),
        P(None, "member", "lon"),
        P(None, "lon"),
    )
    out_specs = (
        P("member", None, "lon"),
        P("member", None, "lon"),
        P(None, "member", "lon"),
        P("member", "lon"),
    )
    return jax.shard_map(
        on_device, mesh=mesh, in_specs=in_specs, out_specs=out_specs, check_vma=False
    )
```

```python
import jax
import jax.numpy as jnp
from jax import lax
from jax.experimental import pallas as pl
from jax.experimental.pallas import tpu as pltpu
from jax.sharding import PartitionSpec as P

MESH = pl.DeviceIdType.MESH

LAT = 64
LEV = 4
SLAB = 512
MEMBERS = 64
STEPS = 2

SOLVE = (13.0, 5.0, 2.0, 1.0)
SOLVE_TWICE = (199.0, 125.0, 71.0, 46.0)
C00 = 0.1 * 13.0 / 21.0
D00 = 0.1 * 199.0 / 441.0

ROWS = (LAT + 2) * 8
XY = [(a, b) for a in (2, 1, 3, 0) for b in (2, 1, 3, 0) if a or b]


def kernel(
    temp_hbm, humid_hbm, wind_hbm, coef_hbm, sst_hbm, ice_hbm, cur_hbm, mask_hbm,
    out_temp_hbm, out_humid_hbm, flux_ref, sst_new_ref,
    temp, humid, wind, mask, own_cur, own_sst, own_ice, coef_ref,
    x0, xp, xq, bp, bq, a1, a2p, a2q, h1, drag, gap, final, uv, ce, cn, m1, m2,
    gathered, stress, heat, got, part, got_z, edge, edge_in, rim, rim_in, rim_z, rim_xy, out_temp, out_humid,
    in_sem, out_sem, z_send, z_recv, xy_send, xy_recv, lon_send, lon_recv, rim_send, rim_recv, rimxy_send, rimxy_recv, red_send, red_recv, redz_send, redz_recv,
):
    m = lax.axis_index("member")
    lon = lax.axis_index("lon")
    x, z, y = m // 16, (m // 4) % 4, m % 4

    def z_peer(d):
        return (x * 16 + ((z + d) % 4) * 4 + y, lon)

    def xy_peer(a, b):
        return (((x + a) % 4) * 16 + z * 4 + (y + b) % 4, lon)

    def lon_peer(d):
        return (m, (lon + d) % 4)

    def rim_peer(d, s):
        return (x * 16 + ((z + d) % 4) * 4 + y, (lon + s) % 4)

    barrier = pltpu.get_barrier_semaphore()
    peers = (
        [z_peer(d) for d in (2, 1, 3)]
        + [xy_peer(a, b) for a, b in XY]
        + [rim_peer(d, s) for d in (2, 1, 3, 0) for s in (1, 3)]
    )
    for peer in peers:
        pl.semaphore_signal(barrier, inc=1, device_id=peer, device_id_type=MESH)

    loads = [
        pltpu.make_async_copy(src, dst, in_sem.at[i])
        for i, (src, dst) in enumerate(
            [
                (cur_hbm, own_cur),
                (sst_hbm, own_sst),
                (ice_hbm, own_ice),
                (wind_hbm, wind),
                (temp_hbm, temp),
                (humid_hbm, humid),
                (mask_hbm, mask),
                (coef_hbm, coef_ref),
            ]
        )
    ]
    for copy in loads:
        copy.start()

    def remote(src, dst, send, recv, peer):
        return pltpu.make_async_remote_copy(
            src_ref=src, dst_ref=dst, send_sem=send, recv_sem=recv, device_id=peer, device_id_type=MESH
        )

    sub = lax.broadcasted_iota(jnp.int32, (8, 128), 0)
    lane = lax.broadcasted_iota(jnp.int32, (8, 128), 1)
    first_run = (sub % 4) == 0
    last_run = (sub % 4) == 3
    upper = sub < 4
    lane_first = lane == 0
    lane_last = lane == 127
    second_slot_of = jnp.where(first_run, (lane + 127) % 128, jnp.where(last_run, (lane + 2) % 128, -1))
    slot_of = jnp.where(first_run, lane, jnp.where(last_run, (lane + 1) % 128, -1))

    def spread(ref, start, value):
        for c in range(4):
            ref[pl.ds(start + c, 8, stride=8), :] = value[:, c * 128 : (c + 1) * 128]

    def rows_of(ref, j0, shift=1, n=8):
        return ref[pl.ds(pl.multiple_of((j0 + shift) * 8, 8), 8 * n), :].reshape(n, 8, 128)

    def put(ref, j0, value):
        n = value.shape[0]
        ref[pl.ds(pl.multiple_of((j0 + 1) * 8, 8), 8 * n), :] = value.reshape(8 * n, 128)

    def close(ref):
        ref[0:8, :] = ref[8:16, :]
        ref[ROWS - 8 : ROWS, :] = ref[ROWS - 16 : ROWS - 8, :]

    def pack(packed, j0, tiles):
        for k in range(len(tiles)):
            packed = jnp.where(slot_of == j0 + k, pltpu.roll(tiles[k], j0 + k, 1), packed)
        return packed

    def pack_two(packed, second, j0, tiles):
        for k in range(len(tiles)):
            turned = pltpu.roll(tiles[k], j0 + k, 1)
            packed = jnp.where(slot_of == j0 + k, turned, packed)
            second = jnp.where(second_slot_of == j0 + k, turned, second)
        return packed, second

    def align(second):
        return jnp.where(first_run, pltpu.roll(second, 127, 1), pltpu.roll(second, 1, 1))

    def advect_halo(centre, inner, outer, eastward, northward):
        west = jnp.where(first_run, outer, inner)
        east = jnp.where(first_run, inner, outer)
        north = jnp.where(slot_of == LAT - 1, centre, pltpu.roll(centre, 127, 1))
        south = jnp.where(slot_of == 0, centre, pltpu.roll(centre, 1, 1))
        return 0.2 * centre + 0.4 * (west + south) + eastward * (east - west) + northward * (north - south)

    def join(west, east):
        from_west = pltpu.roll(pltpu.roll(west, 5, 0), 1, 1)
        from_east = pltpu.roll(pltpu.roll(east, 3, 0), 127, 1)
        return jnp.where(first_run, from_west, from_east)

    def merge(i):
        return join(edge_in[0, i], edge_in[1, i])

    def advect(ref, j0, halo, n=8):
        centre, north, south = (rows_of(ref, j0, shift, n) for shift in (1, 2, 0))
        eastward, northward = rows_of(ce, j0, 1, n), rows_of(cn, j0, 1, n)
        result = []
        for k in range(n):
            c = centre[k]
            own_halo = pltpu.roll(halo, (128 - (j0 + k)) % 128, 1)
            right = pltpu.roll(c, 1, 1)
            left = pltpu.roll(c, 127, 1)
            west = jnp.where(lane_first, jnp.where(first_run, own_halo, pltpu.roll(right, 1, 0)), right)
            east = jnp.where(lane_last, jnp.where(last_run, own_halo, pltpu.roll(left, 7, 0)), left)
            result.append(
                0.2 * c
                + 0.4 * (west + south[k])
                + eastward[k] * (east - west)
                + northward[k] * (north[k] - south[k])
            )
        return jnp.stack(result)

    for copy in loads[:3]:
        copy.wait()
    gathered[x, z, y, 0:8, :] = own_cur[...]
    gathered[x, z, y, 8:12, :] = own_sst[...]
    gathered[x, z, y, 12:16, :] = own_ice[...]

    def own_slots(tile):
        return jnp.where(slot_of == m, pltpu.roll(tile, m, 1), 0.0)

    rim_tile = own_slots(gathered[x, z, y, 8:16, :])
    rim[...] = (
        own_slots(own_cur[...])
        + pltpu.roll(jnp.where(first_run, rim_tile, 0.0), 1, 0)
        + pltpu.roll(jnp.where(last_run, rim_tile, 0.0), 7, 0)
    )

    pl.semaphore_wait(barrier, len(peers))

    sends = []

    def begin(copy):
        copy.start()
        sends.append(copy)
        return copy

    def forward(i, row_z):
        row = gathered.at[x, row_z, y]
        return [
            begin(remote(row, row, xy_send.at[i, n], xy_recv.at[i, n], xy_peer(a, b)))
            for n, (a, b) in enumerate(XY)
        ]

    def exchange(first, count, turn):
        return [
            begin(
                remote(
                    edge.at[pl.ds(first, count)],
                    edge_in.at[s, pl.ds(first, count)],
                    lon_send.at[turn, s],
                    lon_recv.at[turn, s],
                    lon_peer(d),
                )
            )
            for s, d in ((0, 1), (1, 3))
        ]

    own_row = gathered.at[x, z, y]
    along_z = {
        d: begin(remote(own_row, own_row, z_send.at[d - 1], z_recv.at[d - 1], z_peer(d))) for d in (2, 1, 3)
    }
    rims = [
        begin(remote(rim, rim_in.at[s, d], rim_send.at[s, d], rim_recv.at[s, d], rim_peer(d, shift)))
        for d in (2, 1, 3, 0)
        for s, shift in ((0, 1), (1, 3))
    ]
    gathers = [forward(0, z)]

    for copy in loads[3:6]:
        copy.wait()

    def prepare(i, carry):
        r0 = pl.multiple_of(i * 16, 16)
        for f, source in ((0, temp), (1, humid)):
            levels = [source[0, k, pl.ds(r0, 16), :].astype(jnp.float32) for k in range(LEV)]
            once = sum(SOLVE[k] * levels[k] for k in range(LEV)) * (1.0 / 21.0)
            twice = sum(SOLVE_TWICE[k] * levels[k] for k in range(LEV)) * (1.0 / 441.0)
            for h in range(2):
                start = (r0 + 8 * h + 1) * 8 + 4 * f
                for ref, value in ((x0, levels[0]), (xp, once), (xq, twice)):
                    spread(ref, start, value[8 * h : 8 * h + 8])
        u = wind[0, 0, pl.ds(r0, 16), :].astype(jnp.float32)
        v = wind[0, 1, pl.ds(r0, 16), :].astype(jnp.float32)
        for h in range(2):
            start = (r0 + 8 * h + 1) * 8
            own = slice(8 * h, 8 * h + 8)
            spread(uv, start, u[own])
            spread(uv, start + 4, v[own])
            for f in range(2):
                spread(ce, start + 4 * f, 0.2 - 0.1 * u[own])
                spread(cn, start + 4 * f, 0.2 - 0.1 * v[own])
        return carry

    lax.fori_loop(0, LAT // 16, prepare, 0)
    for ref in (x0, xp, xq):
        close(ref)

    loads[6].wait()
    loads[7].wait()

    def masks(i, carry):
        r0 = pl.multiple_of(i * 8, 8)
        kind = mask[pl.ds(r0, 8), :]
        start = (r0 + 1) * 8
        sea = jnp.where((kind == 1) | (kind == 2), 1.0, 0.0)
        icy = jnp.where(kind == 2, 1.0, 0.0)
        for f in range(2):
            spread(m1, start + 4 * f, sea)
            spread(m2, start + 4 * f, icy)
        return carry

    lax.fori_loop(0, LAT // 8, masks, 0)

    def pack_inputs(i, packed):
        j0 = i * 8
        first, first2 = pack_two(packed[0], packed[7], j0, rows_of(x0, j0))
        p, p2 = pack_two(packed[1], packed[2], j0, rows_of(xp, j0))
        q, q2 = pack_two(packed[3], packed[4], j0, rows_of(xq, j0))
        east, north, winds, sea, icy = (
            pack(packed[t], j0, rows_of(ref, j0)) for t, ref in ((5, ce), (6, cn), (8, uv), (9, m1), (10, m2))
        )
        return first, p, p2, q, q2, east, north, first2, winds, sea, icy

    zero = jnp.zeros((8, 128), jnp.float32)
    packed = lax.fori_loop(0, LAT // 8, pack_inputs, (zero,) * 11)
    for i in range(11):
        edge[i] = align(packed[i]) if i in (2, 4, 7) else packed[i]

    halos = exchange(0, 11, 0)

    for i, d in ((1, 1), (2, 3), (3, 2)):
        along_z[d].wait_recv()
        gathers.append(forward(i, (z - d + 4) % 4))

    for copy in rims:
        copy.wait_recv()
    west_rim, east_rim = (sum(rim_in[s, d] for d in range(4)) for s in range(2))
    rim_z[...] = jnp.where((sub % 4) >= 2, west_rim, east_rim)
    rims = [
        begin(remote(rim_z, rim_xy.at[n], rimxy_send.at[n], rimxy_recv.at[n], xy_peer(a, b)))
        for n, (a, b) in enumerate(XY)
    ]

    for copy in halos:
        copy.wait_recv()
    halo = [merge(i) for i in range(11)]
    halo_bp = advect_halo(halo[1], edge[1], halo[2], halo[5], halo[6])
    halo_a1 = advect_halo(halo[0], edge[0], halo[7], halo[5], halo[6])
    halo_bq = advect_halo(halo[3], edge[3], halo[4], halo[5], halo[6])

    def first_step(i, carry):
        j0 = i * 8
        put(a1, j0, advect(x0, j0, halo[0]))
        put(bp, j0, advect(xp, j0, halo[1]))
        put(bq, j0, advect(xq, j0, halo[3]))
        return carry

    lax.fori_loop(0, LAT // 8, first_step, 0)
    close(bp)
    close(bq)

    def second_step(i, carry):
        j0 = i * 8
        put(a2p, j0, advect(bp, j0, halo_bp))
        put(a2q, j0, advect(bq, j0, halo_bq))
        return carry

    lax.fori_loop(0, LAT // 8, second_step, 0)

    coef = coef_ref[0]

    def forcing(winds, currents, tile, sea, icy):
        rel = winds - currents
        turned = pltpu.roll(tile, 4, 0)
        target = jnp.where(upper, tile, 0.5 * turned)
        ice = jnp.where(upper, turned, tile)
        square = rel * rel
        speed = jnp.sqrt(square + pltpu.roll(square, 4, 0) + 1.0)
        return rel, target, coef * speed * (sea - icy * ice)

    def fluxes(row_z):
        def step(ix, carry):
            j0 = ix * 16 + row_z * 4
            block = gathered[ix, row_z]
            winds, one_step, two_steps, sea, icy = (rows_of(ref, j0, 1, 4) for ref in (uv, a1, a2p, m1, m2))
            drags, gaps, stresses, heats = [], [], [], []
            for k in range(4):
                rel, target, d = forcing(winds[k], block[k, 0:8], block[k, 8:16], sea[k], icy[k])
                drags.append(d)
                stresses.append(2.0 * d * rel)
                gaps.append(target - two_steps[k])
                heats.append(d * (target - one_step[k]))
            put(drag, j0, jnp.stack(drags))
            put(gap, j0, jnp.stack(gaps))
            put(h1, j0, jnp.stack(heats))
            stress[ix, row_z] = jnp.stack(stresses)
            return carry

        return step

    def scatter(k, source, d):
        return [
            begin(
                remote(
                    source.at[(x + a) % 4, (z + d) % 4, (y + b) % 4],
                    got.at[k, d, n],
                    red_send.at[k, d, n],
                    red_recv.at[k, d, n],
                    xy_peer(a, b),
                )
            )
            for n, (a, b) in enumerate(XY)
        ]

    def reduce(k, source, copies, d):
        total = source[x, (z + d) % 4, y]
        for n, copy in enumerate(copies):
            copy.wait_recv()
            total = total + got[k, d, n]
        part[k, d] = total
        if d:
            return begin(
                remote(part.at[k, d], got_z.at[k, d - 1], redz_send.at[k, d - 1], redz_recv.at[k, d - 1], z_peer(d))
            )

    def owned(k, copies):
        total = part[k, 0]
        for d in (1, 3, 2):
            copies[d].wait_recv()
            total = total + got_z[k, d - 1]
        return total * (1.0 / (MEMBERS * STEPS))

    stress_copies, heat_copies, stress_z, heat_z = {}, {}, {}, {}
    for copies, d in zip(gathers, (0, 3, 1, 2)):
        for copy in copies:
            copy.wait_recv()
        lax.fori_loop(0, 4, fluxes((z + d) % 4), 0, unroll=True)
        stress_copies[d] = scatter(0, stress, d)
    close(h1)

    far = rim_z[...]
    for n, copy in enumerate(rims):
        copy.wait_recv()
        far = far + rim_xy[n]
    far_tile = jnp.where(first_run, pltpu.roll(far, 7, 0), pltpu.roll(far, 1, 0))
    _, target, d_halo = forcing(halo[8], join(far, far), join(far_tile, far_tile), halo[9], halo[10])
    halo_h = d_halo * (target - halo_a1)

    def last_step(row_z):
        def step(ix, carry):
            j0 = ix * 16 + row_z * 4
            moved = advect(h1, j0, halo_h, 4)
            second = rows_of(drag, j0, 1, 4) * (rows_of(gap, j0, 1, 4) - C00 * moved)
            heat[ix, row_z] = rows_of(h1, j0, 1, 4) + second
            put(final, j0, rows_of(a2q, j0, 1, 4) + D00 * moved + C00 * second)
            return carry

        return step

    for d in (2, 1, 3, 0):
        lax.fori_loop(0, 4, last_step((z + d) % 4), 0, unroll=True)
        heat_copies[d] = scatter(1, heat, d)

    def unspread(i, carry):
        r0 = pl.multiple_of(i * 8, 8)
        for f, target in ((0, out_temp_hbm), (1, out_humid_hbm)):
            for c in range(4):
                target[0, pl.ds(r0, 8), c * 128 : (c + 1) * 128] = final[
                    pl.ds((r0 + 1) * 8 + 4 * f + c, 8, stride=8), :
                ]
        return carry

    lax.fori_loop(0, LAT // 8, unspread, 0)
    for d in (0, 3, 1):
        stress_z[d] = reduce(0, stress, stress_copies[d], d)
    early, sends[:] = sends[:], []
    for copy in early:
        copy.wait_send()
    for d in (2, 1, 3, 0):
        heat_z[d] = reduce(1, heat, heat_copies[d], d)
        if d == 2:
            stress_z[d] = reduce(0, stress, stress_copies[d], d)
    flux_ref[8:16, :] = owned(0, stress_z)
    warm = owned(1, heat_z)
    flux_ref[0:8, :] = warm
    sst_new_ref[...] = own_sst[...] - 0.5 * warm[0:4, :]
    for copy in sends:
        copy.wait_send()


def hand_over(*refs):
    for source, target in zip(refs[:4], refs[4:]):
        target[...] = source[...]


def on_device(
    air_temp, air_humid, wind, exchange_coef, sea_surface_anomaly, sea_ice, current, surface_mask
):
    f32 = jnp.float32
    tall = pltpu.VMEM((ROWS, 128), f32)
    dma = pltpu.SemaphoreType.DMA
    any_space = pl.BlockSpec(memory_space=pl.ANY)
    vmem = pl.BlockSpec(memory_space=pltpu.VMEM)

    out_shape = (
        jax.ShapeDtypeStruct((1, LAT, SLAB), f32),
        jax.ShapeDtypeStruct((1, LAT, SLAB), f32),
        jax.ShapeDtypeStruct((16, 128), f32),
        jax.ShapeDtypeStruct((4, 128), f32),
    )
    results = pl.pallas_call(
        kernel,
        out_shape=tuple(pltpu.VMEM(o.shape, o.dtype) for o in out_shape),
        in_specs=[any_space] * 3 + [pl.BlockSpec(memory_space=pltpu.HBM)] + [any_space] * 4,
        out_specs=(vmem, vmem, vmem, vmem),
        scratch_shapes=[
            pltpu.VMEM((1, LEV, LAT, SLAB), jnp.bfloat16),
            pltpu.VMEM((1, LEV, LAT, SLAB), jnp.bfloat16),
            pltpu.VMEM((1, 2, LAT, SLAB), jnp.bfloat16),
            pltpu.VMEM((LAT, SLAB), jnp.int32),
            pltpu.VMEM((8, 128), f32),
            pltpu.VMEM((4, 128), f32),
            pltpu.VMEM((4, 128), f32),
            pltpu.SMEM((1,), f32),
        ]
        + [tall] * 17
        + [
            pltpu.VMEM((4, 4, 4, 16, 128), f32),
            pltpu.VMEM((4, 4, 4, 8, 128), f32),
            pltpu.VMEM((4, 4, 4, 8, 128), f32),
            pltpu.VMEM((2, 4, 15, 8, 128), f32),
            pltpu.VMEM((2, 4, 8, 128), f32),
            pltpu.VMEM((2, 3, 8, 128), f32),
            pltpu.VMEM((11, 8, 128), f32),
            pltpu.VMEM((2, 11, 8, 128), f32),
            pltpu.VMEM((8, 128), f32),
            pltpu.VMEM((2, 4, 8, 128), f32),
            pltpu.VMEM((8, 128), f32),
            pltpu.VMEM((15, 8, 128), f32),
            pltpu.VMEM((1, LAT, SLAB), f32),
            pltpu.VMEM((1, LAT, SLAB), f32),
            dma((8,)),
            dma((2,)),
            dma((3,)),
            dma((3,)),
            dma((4, 15)),
            dma((4, 15)),
            dma((1, 2)),
            dma((1, 2)),
            dma((2, 4)),
            dma((2, 4)),
            dma((15,)),
            dma((15,)),
            dma((2, 4, 15)),
            dma((2, 4, 15)),
            dma((2, 3)),
            dma((2, 3)),
        ],
        compiler_params=pltpu.CompilerParams(
            collective_id=0, has_side_effects=True, vmem_limit_bytes=56 * 2**20
        ),
        cost_estimate=pl.CostEstimate(flops=20_000_000, bytes_accessed=1_200_000, transcendentals=32_768),
    )(
        air_temp,
        air_humid,
        wind,
        exchange_coef,
        sea_surface_anomaly.reshape(4, 128),
        sea_ice.reshape(4, 128),
        current.reshape(8, 128),
        surface_mask,
    )
    out_temp, out_humid, flux, sst_new = pl.pallas_call(
        hand_over,
        out_shape=out_shape,
        in_specs=[vmem] * 4,
        out_specs=[vmem] * 4,
    )(*[pltpu.with_memory_space_constraint(r, pltpu.VMEM) for r in results])
    return out_temp, out_humid, flux.reshape(4, 1, SLAB), sst_new.reshape(1, SLAB)


def solution(mesh):
    in_specs = (
        P("member", None, None, "lon"),
        P("member", None, None, "lon"),
        P("member", None, None, "lon"),
        P("member"),
        P("member", "lon"),
        P("member", "lon"),
        P(None, "member", "lon"),
        P(None, "lon"),
    )
    out_specs = (
        P("member", None, "lon"),
        P("member", None, "lon"),
        P(None, "member", "lon"),
        P("member", "lon"),
    )
    return jax.shard_map(
        on_device, mesh=mesh, in_specs=in_specs, out_specs=out_specs, check_vma=False
    )
```

```python
import jax
import jax.numpy as jnp
from jax import lax
from jax.experimental import pallas as pl
from jax.experimental.pallas import tpu as pltpu
from jax.sharding import PartitionSpec as P

MESH = pl.DeviceIdType.MESH

LAT = 64
LEV = 4
SLAB = 512
MEMBERS = 64
STEPS = 2

SOLVE = (13.0, 5.0, 2.0, 1.0)
SOLVE_TWICE = (199.0, 125.0, 71.0, 46.0)
C00 = 0.1 * 13.0 / 21.0
D00 = 0.1 * 199.0 / 441.0

ROWS = (LAT + 2) * 8
XY = [(a, b) for a in (2, 1, 3, 0) for b in (2, 1, 3, 0) if a or b]


def kernel(
    temp_hbm, humid_hbm, wind_hbm, coef_hbm, sst_hbm, ice_hbm, cur_hbm, mask_hbm,
    out_temp_hbm, out_humid_hbm, flux_ref, sst_new_ref,
    temp, humid, wind, mask, own_cur, own_sst, own_ice, coef_ref,
    x0, xp, xq, bp, bq, a1, a2p, a2q, h1, drag, gap, final, uv, ce, cn, m1, m2,
    gathered, stress, heat, got, part, got_z, edge, edge_in, rim, rim_in, rim_z, rim_xy, out_temp, out_humid,
    in_sem, out_sem, z_send, z_recv, xy_send, xy_recv, lon_send, lon_recv, rim_send, rim_recv, rimxy_send, rimxy_recv, red_send, red_recv, redz_send, redz_recv,
):
    m = lax.axis_index("member")
    lon = lax.axis_index("lon")
    x, z, y = m // 16, (m // 4) % 4, m % 4

    def z_peer(d):
        return (x * 16 + ((z + d) % 4) * 4 + y, lon)

    def xy_peer(a, b):
        return (((x + a) % 4) * 16 + z * 4 + (y + b) % 4, lon)

    def lon_peer(d):
        return (m, (lon + d) % 4)

    def rim_peer(d, s):
        return (x * 16 + ((z + d) % 4) * 4 + y, (lon + s) % 4)

    barrier = pltpu.get_barrier_semaphore()
    peers = (
        [z_peer(d) for d in (2, 1, 3)]
        + [xy_peer(a, b) for a, b in XY]
        + [rim_peer(d, s) for d in (2, 1, 3, 0) for s in (1, 3)]
    )
    for peer in peers:
        pl.semaphore_signal(barrier, inc=1, device_id=peer, device_id_type=MESH)

    loads = [
        pltpu.make_async_copy(src, dst, in_sem.at[i])
        for i, (src, dst) in enumerate(
            [
                (cur_hbm, own_cur),
                (sst_hbm, own_sst),
                (ice_hbm, own_ice),
                (wind_hbm, wind),
                (temp_hbm, temp),
                (humid_hbm, humid),
                (mask_hbm, mask),
                (coef_hbm, coef_ref),
            ]
        )
    ]
    for copy in loads:
        copy.start()

    def remote(src, dst, send, recv, peer):
        return pltpu.make_async_remote_copy(
            src_ref=src, dst_ref=dst, send_sem=send, recv_sem=recv, device_id=peer, device_id_type=MESH
        )

    sub = lax.broadcasted_iota(jnp.int32, (8, 128), 0)
    lane = lax.broadcasted_iota(jnp.int32, (8, 128), 1)
    first_run = (sub % 4) == 0
    last_run = (sub % 4) == 3
    upper = sub < 4
    lane_first = lane == 0
    lane_last = lane == 127
    second_slot_of = jnp.where(first_run, (lane + 127) % 128, jnp.where(last_run, (lane + 2) % 128, -1))
    slot_of = jnp.where(first_run, lane, jnp.where(last_run, (lane + 1) % 128, -1))

    def spread(ref, start, value):
        for c in range(4):
            ref[pl.ds(start + c, 8, stride=8), :] = value[:, c * 128 : (c + 1) * 128]

    def rows_of(ref, j0, shift=1, n=8):
        return ref[pl.ds(pl.multiple_of((j0 + shift) * 8, 8), 8 * n), :].reshape(n, 8, 128)

    def put(ref, j0, value):
        n = value.shape[0]
        ref[pl.ds(pl.multiple_of((j0 + 1) * 8, 8), 8 * n), :] = value.reshape(8 * n, 128)

    def close(ref):
        ref[0:8, :] = ref[8:16, :]
        ref[ROWS - 8 : ROWS, :] = ref[ROWS - 16 : ROWS - 8, :]

    def pack(packed, j0, tiles):
        for k in range(len(tiles)):
            packed = jnp.where(slot_of == j0 + k, pltpu.roll(tiles[k], j0 + k, 1), packed)
        return packed

    def pack_two(packed, second, j0, tiles):
        for k in range(len(tiles)):
            turned = pltpu.roll(tiles[k], j0 + k, 1)
            packed = jnp.where(slot_of == j0 + k, turned, packed)
            second = jnp.where(second_slot_of == j0 + k, turned, second)
        return packed, second

    def align(second):
        return jnp.where(first_run, pltpu.roll(second, 127, 1), pltpu.roll(second, 1, 1))

    def advect_halo(centre, inner, outer, eastward, northward):
        west = jnp.where(first_run, outer, inner)
        east = jnp.where(first_run, inner, outer)
        north = jnp.where(slot_of == LAT - 1, centre, pltpu.roll(centre, 127, 1))
        south = jnp.where(slot_of == 0, centre, pltpu.roll(centre, 1, 1))
        return 0.2 * centre + 0.4 * (west + south) + eastward * (east - west) + northward * (north - south)

    def join(west, east):
        from_west = pltpu.roll(pltpu.roll(west, 5, 0), 1, 1)
        from_east = pltpu.roll(pltpu.roll(east, 3, 0), 127, 1)
        return jnp.where(first_run, from_west, from_east)

    def merge(i):
        return join(edge_in[0, i], edge_in[1, i])

    def advect(ref, j0, halo, n=8):
        centre, north, south = (rows_of(ref, j0, shift, n) for shift in (1, 2, 0))
        eastward, northward = rows_of(ce, j0, 1, n), rows_of(cn, j0, 1, n)
        result = []
        for k in range(n):
            c = centre[k]
            own_halo = pltpu.roll(halo, (128 - (j0 + k)) % 128, 1)
            right = pltpu.roll(c, 1, 1)
            left = pltpu.roll(c, 127, 1)
            west = jnp.where(lane_first, jnp.where(first_run, own_halo, pltpu.roll(right, 1, 0)), right)
            east = jnp.where(lane_last, jnp.where(last_run, own_halo, pltpu.roll(left, 7, 0)), left)
            result.append(
                0.2 * c
                + 0.4 * (west + south[k])
                + eastward[k] * (east - west)
                + northward[k] * (north[k] - south[k])
            )
        return jnp.stack(result)

    for copy in loads[:3]:
        copy.wait()
    gathered[x, z, y, 0:8, :] = own_cur[...]
    gathered[x, z, y, 8:12, :] = own_sst[...]
    gathered[x, z, y, 12:16, :] = own_ice[...]

    def own_slots(tile):
        return jnp.where(slot_of == m, pltpu.roll(tile, m, 1), 0.0)

    rim_tile = own_slots(gathered[x, z, y, 8:16, :])
    rim[...] = (
        own_slots(own_cur[...])
        + pltpu.roll(jnp.where(first_run, rim_tile, 0.0), 1, 0)
        + pltpu.roll(jnp.where(last_run, rim_tile, 0.0), 7, 0)
    )

    pl.semaphore_wait(barrier, len(peers))

    sends = []

    def begin(copy):
        copy.start()
        sends.append(copy)
        return copy

    def forward(i, row_z):
        row = gathered.at[x, row_z, y]
        return [
            begin(remote(row, row, xy_send.at[i, n], xy_recv.at[i, n], xy_peer(a, b)))
            for n, (a, b) in enumerate(XY)
        ]

    def exchange(first, count, turn):
        return [
            begin(
                remote(
                    edge.at[pl.ds(first, count)],
                    edge_in.at[s, pl.ds(first, count)],
                    lon_send.at[turn, s],
                    lon_recv.at[turn, s],
                    lon_peer(d),
                )
            )
            for s, d in ((0, 1), (1, 3))
        ]

    own_row = gathered.at[x, z, y]
    along_z = {
        d: begin(remote(own_row, own_row, z_send.at[d - 1], z_recv.at[d - 1], z_peer(d))) for d in (2, 1, 3)
    }
    rims = [
        begin(remote(rim, rim_in.at[s, d], rim_send.at[s, d], rim_recv.at[s, d], rim_peer(d, shift)))
        for d in (2, 1, 3, 0)
        for s, shift in ((0, 1), (1, 3))
    ]
    gathers = [forward(0, z)]

    for copy in loads[3:6]:
        copy.wait()

    def prepare(i, carry):
        r0 = pl.multiple_of(i * 16, 16)
        for f, source in ((0, temp), (1, humid)):
            levels = [source[0, k, pl.ds(r0, 16), :].astype(jnp.float32) for k in range(LEV)]
            once = sum(SOLVE[k] * levels[k] for k in range(LEV)) * (1.0 / 21.0)
            twice = sum(SOLVE_TWICE[k] * levels[k] for k in range(LEV)) * (1.0 / 441.0)
            for h in range(2):
                start = (r0 + 8 * h + 1) * 8 + 4 * f
                for ref, value in ((x0, levels[0]), (xp, once), (xq, twice)):
                    spread(ref, start, value[8 * h : 8 * h + 8])
        u = wind[0, 0, pl.ds(r0, 16), :].astype(jnp.float32)
        v = wind[0, 1, pl.ds(r0, 16), :].astype(jnp.float32)
        for h in range(2):
            start = (r0 + 8 * h + 1) * 8
            own = slice(8 * h, 8 * h + 8)
            spread(uv, start, u[own])
            spread(uv, start + 4, v[own])
            for f in range(2):
                spread(ce, start + 4 * f, 0.2 - 0.1 * u[own])
                spread(cn, start + 4 * f, 0.2 - 0.1 * v[own])
        return carry

    lax.fori_loop(0, LAT // 16, prepare, 0)
    for ref in (x0, xp, xq):
        close(ref)

    loads[6].wait()
    loads[7].wait()

    def masks(i, carry):
        r0 = pl.multiple_of(i * 8, 8)
        kind = mask[pl.ds(r0, 8), :]
        start = (r0 + 1) * 8
        sea = jnp.where((kind == 1) | (kind == 2), 1.0, 0.0)
        icy = jnp.where(kind == 2, 1.0, 0.0)
        for f in range(2):
            spread(m1, start + 4 * f, sea)
            spread(m2, start + 4 * f, icy)
        return carry

    lax.fori_loop(0, LAT // 8, masks, 0)

    def pack_inputs(i, packed):
        j0 = i * 8
        first, first2 = pack_two(packed[0], packed[7], j0, rows_of(x0, j0))
        p, p2 = pack_two(packed[1], packed[2], j0, rows_of(xp, j0))
        q, q2 = pack_two(packed[3], packed[4], j0, rows_of(xq, j0))
        east, north, winds, sea, icy = (
            pack(packed[t], j0, rows_of(ref, j0)) for t, ref in ((5, ce), (6, cn), (8, uv), (9, m1), (10, m2))
        )
        return first, p, p2, q, q2, east, north, first2, winds, sea, icy

    zero = jnp.zeros((8, 128), jnp.float32)
    packed = lax.fori_loop(0, LAT // 8, pack_inputs, (zero,) * 11)
    for i in range(11):
        edge[i] = align(packed[i]) if i in (2, 4, 7) else packed[i]

    halos = exchange(0, 11, 0)

    for i, d in ((1, 1), (2, 3)):
        along_z[d].wait_recv()
        gathers.append(forward(i, (z - d + 4) % 4))

    for copy in rims:
        copy.wait_recv()
    west_rim, east_rim = (sum(rim_in[s, d] for d in range(4)) for s in range(2))
    rim_z[...] = jnp.where((sub % 4) >= 2, west_rim, east_rim)
    rims = [
        begin(remote(rim_z, rim_xy.at[n], rimxy_send.at[n], rimxy_recv.at[n], xy_peer(a, b)))
        for n, (a, b) in enumerate(XY)
    ]

    along_z[2].wait_recv()
    gathers.append(forward(3, (z + 2) % 4))


    for copy in halos:
        copy.wait_recv()
    halo = [merge(i) for i in range(11)]
    halo_bp = advect_halo(halo[1], edge[1], halo[2], halo[5], halo[6])
    halo_a1 = advect_halo(halo[0], edge[0], halo[7], halo[5], halo[6])
    halo_bq = advect_halo(halo[3], edge[3], halo[4], halo[5], halo[6])

    def first_step(i, carry):
        j0 = i * 8
        put(a1, j0, advect(x0, j0, halo[0]))
        put(bp, j0, advect(xp, j0, halo[1]))
        put(bq, j0, advect(xq, j0, halo[3]))
        return carry

    lax.fori_loop(0, LAT // 8, first_step, 0)
    close(bp)
    close(bq)

    def second_step(i, carry):
        j0 = i * 8
        put(a2p, j0, advect(bp, j0, halo_bp))
        put(a2q, j0, advect(bq, j0, halo_bq))
        return carry

    lax.fori_loop(0, LAT // 8, second_step, 0)

    coef = coef_ref[0]

    def forcing(winds, currents, tile, sea, icy):
        rel = winds - currents
        turned = pltpu.roll(tile, 4, 0)
        target = jnp.where(upper, tile, 0.5 * turned)
        ice = jnp.where(upper, turned, tile)
        square = rel * rel
        speed = jnp.sqrt(square + pltpu.roll(square, 4, 0) + 1.0)
        return rel, target, coef * speed * (sea - icy * ice)

    def fluxes(row_z):
        def step(ix, carry):
            j0 = ix * 16 + row_z * 4
            block = gathered[ix, row_z]
            winds, one_step, two_steps, sea, icy = (rows_of(ref, j0, 1, 4) for ref in (uv, a1, a2p, m1, m2))
            drags, gaps, stresses, heats = [], [], [], []
            for k in range(4):
                rel, target, d = forcing(winds[k], block[k, 0:8], block[k, 8:16], sea[k], icy[k])
                drags.append(d)
                stresses.append(2.0 * d * rel)
                gaps.append(target - two_steps[k])
                heats.append(d * (target - one_step[k]))
            put(drag, j0, jnp.stack(drags))
            put(gap, j0, jnp.stack(gaps))
            put(h1, j0, jnp.stack(heats))
            stress[ix, row_z] = jnp.stack(stresses)
            return carry

        return step

    def scatter(k, source, d):
        return [
            begin(
                remote(
                    source.at[(x + a) % 4, (z + d) % 4, (y + b) % 4],
                    got.at[k, d, n],
                    red_send.at[k, d, n],
                    red_recv.at[k, d, n],
                    xy_peer(a, b),
                )
            )
            for n, (a, b) in enumerate(XY)
        ]

    def reduce(k, source, copies, d):
        total = source[x, (z + d) % 4, y]
        for n, copy in enumerate(copies):
            copy.wait_recv()
            total = total + got[k, d, n]
        part[k, d] = total
        if d:
            return begin(
                remote(part.at[k, d], got_z.at[k, d - 1], redz_send.at[k, d - 1], redz_recv.at[k, d - 1], z_peer(d))
            )

    def owned(k, copies):
        total = part[k, 0]
        for d in (1, 3, 2):
            copies[d].wait_recv()
            total = total + got_z[k, d - 1]
        return total * (1.0 / (MEMBERS * STEPS))

    stress_copies, heat_copies, stress_z, heat_z = {}, {}, {}, {}
    for copies, d in zip(gathers, (0, 3, 1, 2)):
        for copy in copies:
            copy.wait_recv()
        lax.fori_loop(0, 4, fluxes((z + d) % 4), 0, unroll=True)
        stress_copies[d] = scatter(0, stress, d)
    close(h1)

    far = rim_z[...]
    for n, copy in enumerate(rims):
        copy.wait_recv()
        far = far + rim_xy[n]
    far_tile = jnp.where(first_run, pltpu.roll(far, 7, 0), pltpu.roll(far, 1, 0))
    _, target, d_halo = forcing(halo[8], join(far, far), join(far_tile, far_tile), halo[9], halo[10])
    halo_h = d_halo * (target - halo_a1)

    def last_step(row_z):
        def step(ix, carry):
            j0 = ix * 16 + row_z * 4
            moved = advect(h1, j0, halo_h, 4)
            second = rows_of(drag, j0, 1, 4) * (rows_of(gap, j0, 1, 4) - C00 * moved)
            heat[ix, row_z] = rows_of(h1, j0, 1, 4) + second
            put(final, j0, rows_of(a2q, j0, 1, 4) + D00 * moved + C00 * second)
            return carry

        return step

    for d in (2, 1, 3, 0):
        lax.fori_loop(0, 4, last_step((z + d) % 4), 0, unroll=True)
        heat_copies[d] = scatter(1, heat, d)

    def unspread(i, carry):
        r0 = pl.multiple_of(i * 8, 8)
        for f, target in ((0, out_temp_hbm), (1, out_humid_hbm)):
            for c in range(4):
                target[0, pl.ds(r0, 8), c * 128 : (c + 1) * 128] = final[
                    pl.ds((r0 + 1) * 8 + 4 * f + c, 8, stride=8), :
                ]
        return carry

    lax.fori_loop(0, LAT // 8, unspread, 0)
    for d in (0, 3, 1, 2):
        stress_z[d] = reduce(0, stress, stress_copies[d], d)
    for d in (2, 1, 3, 0):
        heat_z[d] = reduce(1, heat, heat_copies[d], d)
    early, sends[:] = sends[:], []
    for copy in early:
        copy.wait_send()
    flux_ref[8:16, :] = owned(0, stress_z)
    warm = owned(1, heat_z)
    flux_ref[0:8, :] = warm
    sst_new_ref[...] = own_sst[...] - 0.5 * warm[0:4, :]
    for copy in sends:
        copy.wait_send()


def hand_over(*refs):
    for source, target in zip(refs[:4], refs[4:]):
        target[...] = source[...]


def on_device(
    air_temp, air_humid, wind, exchange_coef, sea_surface_anomaly, sea_ice, current, surface_mask
):
    f32 = jnp.float32
    tall = pltpu.VMEM((ROWS, 128), f32)
    dma = pltpu.SemaphoreType.DMA
    any_space = pl.BlockSpec(memory_space=pl.ANY)
    vmem = pl.BlockSpec(memory_space=pltpu.VMEM)

    out_shape = (
        jax.ShapeDtypeStruct((1, LAT, SLAB), f32),
        jax.ShapeDtypeStruct((1, LAT, SLAB), f32),
        jax.ShapeDtypeStruct((16, 128), f32),
        jax.ShapeDtypeStruct((4, 128), f32),
    )
    results = pl.pallas_call(
        kernel,
        out_shape=tuple(pltpu.VMEM(o.shape, o.dtype) for o in out_shape),
        in_specs=[any_space] * 3 + [pl.BlockSpec(memory_space=pltpu.HBM)] + [any_space] * 4,
        out_specs=(vmem, vmem, vmem, vmem),
        scratch_shapes=[
            pltpu.VMEM((1, LEV, LAT, SLAB), jnp.bfloat16),
            pltpu.VMEM((1, LEV, LAT, SLAB), jnp.bfloat16),
            pltpu.VMEM((1, 2, LAT, SLAB), jnp.bfloat16),
            pltpu.VMEM((LAT, SLAB), jnp.int32),
            pltpu.VMEM((8, 128), f32),
            pltpu.VMEM((4, 128), f32),
            pltpu.VMEM((4, 128), f32),
            pltpu.SMEM((1,), f32),
        ]
        + [tall] * 17
        + [
            pltpu.VMEM((4, 4, 4, 16, 128), f32),
            pltpu.VMEM((4, 4, 4, 8, 128), f32),
            pltpu.VMEM((4, 4, 4, 8, 128), f32),
            pltpu.VMEM((2, 4, 15, 8, 128), f32),
            pltpu.VMEM((2, 4, 8, 128), f32),
            pltpu.VMEM((2, 3, 8, 128), f32),
            pltpu.VMEM((11, 8, 128), f32),
            pltpu.VMEM((2, 11, 8, 128), f32),
            pltpu.VMEM((8, 128), f32),
            pltpu.VMEM((2, 4, 8, 128), f32),
            pltpu.VMEM((8, 128), f32),
            pltpu.VMEM((15, 8, 128), f32),
            pltpu.VMEM((1, LAT, SLAB), f32),
            pltpu.VMEM((1, LAT, SLAB), f32),
            dma((8,)),
            dma((2,)),
            dma((3,)),
            dma((3,)),
            dma((4, 15)),
            dma((4, 15)),
            dma((1, 2)),
            dma((1, 2)),
            dma((2, 4)),
            dma((2, 4)),
            dma((15,)),
            dma((15,)),
            dma((2, 4, 15)),
            dma((2, 4, 15)),
            dma((2, 3)),
            dma((2, 3)),
        ],
        compiler_params=pltpu.CompilerParams(
            collective_id=0, has_side_effects=True, vmem_limit_bytes=56 * 2**20
        ),
        cost_estimate=pl.CostEstimate(flops=20_000_000, bytes_accessed=1_200_000, transcendentals=32_768),
    )(
        air_temp,
        air_humid,
        wind,
        exchange_coef,
        sea_surface_anomaly.reshape(4, 128),
        sea_ice.reshape(4, 128),
        current.reshape(8, 128),
        surface_mask,
    )
    out_temp, out_humid, flux, sst_new = pl.pallas_call(
        hand_over,
        out_shape=out_shape,
        in_specs=[vmem] * 4,
        out_specs=[vmem] * 4,
    )(*[pltpu.with_memory_space_constraint(r, pltpu.VMEM) for r in results])
    return out_temp, out_humid, flux.reshape(4, 1, SLAB), sst_new.reshape(1, SLAB)


def solution(mesh):
    in_specs = (
        P("member", None, None, "lon"),
        P("member", None, None, "lon"),
        P("member", None, None, "lon"),
        P("member"),
        P("member", "lon"),
        P("member", "lon"),
        P(None, "member", "lon"),
        P(None, "lon"),
    )
    out_specs = (
        P("member", None, "lon"),
        P("member", None, "lon"),
        P(None, "member", "lon"),
        P("member", "lon"),
    )
    return jax.shard_map(
        on_device, mesh=mesh, in_specs=in_specs, out_specs=out_specs, check_vma=False
    )
```
